128 devices in a mesh: row: 4 (over z), col: 32 (over x, y, core).
Axes of the slice: x: 4, y: 4, z: 4, core: 2. Of those that a mesh axis runs over, the one named last changes fastest.
Arguments:
- scan: float32 [4096, 32768], P('row', 'col'), may hold values from -6 to 6
- anchors: int32 [2, 8, 32, 2], P(None, 'row', 'col'), may hold values from -1 to 32256, as said below
- targets: int32 [2, 8, 32], P(None, 'row', 'col'), may hold values from 0 to 8
- stem_weight: bfloat16 [7, 7, 1, 64], replicated, may hold values from -0.875 to 0.875
- stem_bias: float32 [64], replicated, may hold values from -3 to 3
- conv1_weight: bfloat16 [3, 3, 64, 64], replicated, may hold values from -0.25 to 0.25
- conv1_bias: float32 [64], replicated, may hold values from -3 to 3
- conv2_weight: bfloat16 [3, 3, 64, 64], replicated, may hold values from -0.25 to 0.25
- conv2_bias: float32 [64], replicated, may hold values from -3 to 3
- head_weight: bfloat16 [64, 9], replicated, may hold values from -0.75 to 0.75
- head_bias: float32 [9], replicated, may hold values from -4 to 4
Outputs:
- saliency: float32 [4096, 32768], P('row', 'col')
- class_scores: float32 [2, 8, 32], P(None, 'row', 'col')
The draws below stay inside these ranges and needn't reach their ends.
Inputs may be any that keep to these rules, and one draw needn't show every extreme that they name: anchors[p, k, c] is the top-left corner (row, column) of a window lying wholly inside the scan, or has row -1 when the slot is empty. Slots r * 2 to (r + 1) * 2 - 1 of tile column c hold only windows whose corner lies in tile (r, c), that is rows r * 1024 to (r + 1) * 1024 - 1 and columns c * 1024 to (c + 1) * 1024 - 1. In every pass some tile holds 2 live windows and some tile column holds 4; no tile column holds more than 4 live windows in a pass. Every tile column has empty slots in every pass, and empty slots have column c * 1024 + 512.
All inputs are finite; a program needn't handle non-finite values.
Results may differ from the reference program's by a relative error of at most 0.0054.
Values may be sent and summed in bfloat16 or wider, within the bound.
A program may use at most 192 MiB of HBM per device.

```python
import jax
import jax.numpy as jnp
from jax import lax

TILE = 1024
WIN = 512
C = 64
CLASSES = 9
PASSES = 2
PER = 1
SLOTS = 2
H = 4096
W = 32768
N_ROW = 4
N_COL = 32


def draw_anchors(key, part):
    key = jax.random.fold_in(key, 11)
    keys = jax.random.split(key, 6)
    passes, tile_rows, slots, tile_cols = (PASSES, N_ROW, SLOTS, N_COL)
    drawn = jax.random.randint(keys[0], (passes, tile_rows, tile_cols), 0, PER + 1)
    column_keys = jax.random.randint(keys[1], (passes, tile_cols), 0, 1 << 20) * tile_cols + jnp.arange(tile_cols, dtype=jnp.int32)[None, :]
    column_rank = jnp.argsort(jnp.argsort(column_keys, axis=1), axis=1)
    defect = column_rank < 3
    hot_row = jax.random.randint(keys[2], (passes, tile_cols), 0, tile_rows)
    row_ids = jnp.arange(tile_rows, dtype=jnp.int32)[None, :, None]
    is_hot = (row_ids == hot_row[:, None, :]) | (row_ids == (hot_row[:, None, :] + 1) % tile_rows)
    counts = jnp.where(defect[:, None, :], jnp.where(is_hot, slots, 0), drawn)
    slot_keys = jax.random.randint(keys[3], (passes, tile_rows, slots, tile_cols), 0, 1 << 20) * slots + jnp.arange(slots, dtype=jnp.int32)[None, None, :, None]
    slot_rank = jnp.argsort(jnp.argsort(slot_keys, axis=2), axis=2)
    is_live = slot_rank < counts[:, :, None, :]
    row_base = jnp.arange(tile_rows, dtype=jnp.int32)[None, :, None, None] * TILE
    col_base = jnp.arange(tile_cols, dtype=jnp.int32)[None, None, None, :] * TILE
    corner_row = row_base + jax.random.randint(keys[4], (passes, tile_rows, slots, tile_cols), 0, TILE)
    corner_row = jnp.minimum(corner_row, tile_rows * TILE - WIN)
    corner_col = col_base + jax.random.randint(keys[5], (passes, tile_rows, slots, tile_cols), 0, TILE)
    corner_col = jnp.minimum(corner_col, tile_cols * TILE - WIN)
    corner_row = jnp.where(is_live, corner_row, -1)
    corner_col = jnp.where(is_live, corner_col, col_base + (TILE - WIN) + jnp.zeros_like(corner_col))
    stacked = jnp.stack([corner_row, corner_col], axis=-1)
    return stacked.reshape(passes, tile_rows * slots, tile_cols, 2).astype(jnp.int32)


def with_ends(values, rng, smallest, high):
    longest = values.shape.index(max(values.shape))
    spots = []
    for shift in (0, 1):
        where = [jax.random.randint(jax.random.fold_in(rng, axis), (), 0, length) for axis, length in enumerate(values.shape)]
        where[longest] = (where[longest] + shift) % values.shape[longest]
        spots.append(tuple(where))
    return values.at[spots[0]].set(smallest).at[spots[1]].set(high)


def shard_levels(stream_key, extent, pieces, least, top_value):
    factor_of = 1.0
    for dim, parts in pieces:
        steps = jax.random.uniform(jax.random.fold_in(jax.random.fold_in(stream_key, 6), dim), (parts,), jnp.float32, least / len(pieces), top_value / len(pieces))
        factor_of = factor_of * jnp.repeat(jnp.exp(steps), extent[dim] // parts).reshape((-1,) + (1,) * (len(extent) - 1 - dim))
    return factor_of


def bell_draw(stream_key, dims, spread, limit, cuts=(), kind=jnp.bfloat16):
    values = spread * jax.random.normal(stream_key, dims, jnp.float32)
    if cuts:
        values = values * shard_levels(stream_key, dims, cuts, -0.22, 0.18)
    return jnp.clip(values, -limit, limit).astype(kind)


def setup_inputs(seed: int = 0) -> dict:
    splits = jax.random.split(jax.random.key(seed), 12)
    scan = bell_draw(splits[0], (H, W), 1.0, 6.0, ((0, 4), (1, 32)), jnp.float32)
    anchors = draw_anchors(jax.random.fold_in(splits[11], 71), 0)
    targets = with_ends(jax.random.randint(splits[2], (PASSES, N_ROW * SLOTS, N_COL), 0, CLASSES), jax.random.fold_in(splits[2], 1), 0, CLASSES - 1).astype(jnp.int32)
    stem_weight = bell_draw(splits[3], (7, 7, 1, C), 49 ** -0.5, 0.875)
    stem_bias = bell_draw(splits[4], (C,), 0.5, 3.0, (), jnp.float32)
    conv1_weight = bell_draw(splits[5], (3, 3, C, C), (9 * C) ** -0.5, 0.25)
    conv1_bias = bell_draw(splits[6], (C,), 0.5, 3.0, (), jnp.float32)
    conv2_weight = bell_draw(splits[7], (3, 3, C, C), (9 * C) ** -0.5, 0.25)
    conv2_bias = bell_draw(splits[8], (C,), 0.5, 3.0, (), jnp.float32)
    head_weight = bell_draw(splits[9], (C, CLASSES), C ** -0.5, 0.75)
    head_bias = bell_draw(splits[10], (CLASSES,), 1.0, 4.0, (), jnp.float32)
    return dict(scan=scan, anchors=anchors, targets=targets, stem_weight=stem_weight, stem_bias=stem_bias, conv1_weight=conv1_weight, conv1_bias=conv1_bias, conv2_weight=conv2_weight, conv2_bias=conv2_bias, head_weight=head_weight, head_bias=head_bias)


def convolve(inputs, kernel, stride, margin):
    result = lax.conv_general_dilated(inputs[None].astype(jnp.float32), kernel.astype(jnp.float32), (stride, stride), ((margin, margin), (margin, margin)), dimension_numbers=("NHWC", "HWIO", "NHWC"), precision=lax.Precision.HIGHEST)
    return result[0]


def turned(kernel):
    return jnp.flip(kernel, (0, 1)).transpose(0, 1, 3, 2)


def gaussian(offset):
    centre = (WIN - 1) / 2.0
    sigma = WIN / 4.0
    return jnp.exp(-(offset - centre) ** 2 / (2.0 * sigma * sigma))


def explain(cutout, target, stem_weight, stem_bias, conv1_weight, conv1_bias, conv2_weight, conv2_bias, head_weight, head_bias):
    stem_map = jax.nn.relu(convolve(cutout[:, :, None], stem_weight, 2, 3) + stem_bias).astype(jnp.bfloat16)
    features_a = lax.reduce_window(stem_map, jnp.array(-jnp.inf, jnp.bfloat16), lax.max, (3, 3, 1), (2, 2, 1), ((1, 1), (1, 1), (0, 0)))
    pre_first = convolve(features_a, conv1_weight, 1, 1) + conv1_bias
    hidden = jax.nn.relu(pre_first).astype(jnp.bfloat16)
    pre_second = features_a.astype(jnp.float32) + convolve(hidden, conv2_weight, 1, 1) + conv2_bias
    activated = jax.nn.relu(pre_second)
    features = jnp.mean(activated, (0, 1))
    onehot = (jnp.arange(CLASSES, dtype=jnp.int32) == target).astype(jnp.float32)
    head_matrix = head_weight.astype(jnp.float32)
    logits = jnp.dot(features, head_matrix, precision=lax.Precision.HIGHEST) + head_bias
    class_logit = jnp.sum(logits * onehot)
    column = jnp.dot(head_matrix, onehot, precision=lax.Precision.HIGHEST)
    side = WIN // 4
    grad_out = (jnp.where(pre_second > 0, column, 0.0) / float(side * side)).astype(jnp.bfloat16)
    grad_hidden = convolve(grad_out, turned(conv2_weight), 1, 1)
    grad_pre = jnp.where(pre_first > 0, grad_hidden, 0.0).astype(jnp.bfloat16)
    grad_input = grad_out.astype(jnp.float32) + convolve(grad_pre, turned(conv1_weight), 1, 1)
    channel_weights = jnp.sum(grad_input, (0, 1))
    class_map = jax.nn.relu(jnp.einsum("ijk,k->ij", features_a.astype(jnp.float32), channel_weights, precision=lax.Precision.HIGHEST))
    upsampled = jnp.repeat(jnp.repeat(class_map, 4, 0), 4, 1)
    profile = gaussian(jnp.arange(WIN, dtype=jnp.int32).astype(jnp.float32))
    return upsampled * profile[:, None] * profile[None, :], class_logit


def reference(scan, anchors, targets, stem_weight, stem_bias, conv1_weight, conv1_bias, conv2_weight, conv2_bias, head_weight, head_bias):
    pixels = scan.astype(jnp.bfloat16)
    corner_list = anchors.reshape(-1, 2)
    target_list = targets.reshape(-1)
    profile = gaussian(jnp.arange(WIN, dtype=jnp.int32).astype(jnp.float32))
    weight_tile = profile[:, None] * profile[None, :]

    def handle(carried, slot_item):
        summed, weights_sum = carried
        corner, target = slot_item
        is_live = corner[0] >= 0
        start_row = jnp.maximum(corner[0], 0).astype(jnp.int32)
        start_col = corner[1].astype(jnp.int32)
        cutout = lax.dynamic_slice(pixels, (start_row, start_col), (WIN, WIN))

        def compute(window_px):
            return explain(window_px, target, stem_weight, stem_bias, conv1_weight, conv1_bias, conv2_weight, conv2_bias, head_weight, head_bias)

        def empty(window_px):
            return jnp.zeros((WIN, WIN), jnp.float32), jnp.zeros((), jnp.float32)

        contrib, class_logit = lax.cond(is_live, compute, empty, cutout)
        existing = lax.dynamic_slice(summed, (start_row, start_col), (WIN, WIN))
        summed = lax.dynamic_update_slice(summed, existing + contrib, (start_row, start_col))
        existing = lax.dynamic_slice(weights_sum, (start_row, start_col), (WIN, WIN))
        weights_sum = lax.dynamic_update_slice(weights_sum, existing + jnp.where(is_live, weight_tile, 0.0), (start_row, start_col))
        return (summed, weights_sum), class_logit

    blank = jnp.zeros(scan.shape, jnp.float32)
    (summed, weights_sum), logits = lax.scan(handle, (blank, blank), (corner_list, target_list))
    saliency = summed / jnp.maximum(weights_sum, 1.0)
    return saliency, logits.reshape(targets.shape)
```

```python
import jax
import jax.numpy as jnp
from jax import lax
from jax.experimental import pallas as pl
from jax.experimental.pallas import tpu as pltpu
from jax.sharding import PartitionSpec as P

WIN = 512
C = 64
F = 128
LOW = -3.0e38


def arranged(stem_weight, conv1_weight, conv2_weight):
    rows = jnp.arange(8)[:, None, None] * 2 + jnp.arange(7)[None, None, :]
    row_tap = (rows == jnp.arange(24)[None, :, None]).astype(jnp.float32)
    cols = jnp.arange(2)[:, None, None] * 2 + jnp.arange(7)[None, None, :]
    col_tap = (cols == jnp.arange(9)[None, :, None]).astype(jnp.float32)
    kernel = stem_weight[:, :, 0, :].astype(jnp.float32)
    part = jnp.einsum("rty,yxo->rtxo", row_tap, kernel)
    stem = jnp.einsum("qux,rtxo->rqout", col_tap, part)
    stem = stem.reshape(8 * 2 * C, 9 * 24).astype(jnp.bfloat16)
    first = conv1_weight.transpose(0, 3, 1, 2).reshape(3 * C, 3 * C)
    second = conv2_weight.transpose(0, 3, 1, 2).reshape(3 * C, 3 * C)
    back = jnp.flip(conv2_weight, (0, 1)).transpose(0, 2, 1, 3).reshape(3 * C, 3 * C)
    sums = jnp.flip(conv1_weight, (0, 1)).transpose(0, 1, 3, 2).reshape(9, C, C)
    return stem, first, second, back, sums.astype(jnp.float32)


def lanes(shape):
    return lax.broadcasted_iota(jnp.int32, shape, len(shape) - 1)


def put_taps(ref, row, value):
    lane = lanes((C, F))
    left = jnp.where(lane == 0, 0.0, pltpu.roll(value, 1, 1))
    right = jnp.where(lane == F - 1, 0.0, pltpu.roll(value, F - 1, 1))
    ref[row, 0:C, :] = left.astype(jnp.bfloat16)
    ref[row, C : 2 * C, :] = value.astype(jnp.bfloat16)
    ref[row, 2 * C : 3 * C, :] = right.astype(jnp.bfloat16)


def convolved(taps_ref, weight_ref, finish, state):
    weight = weight_ref[...]
    zero = jnp.zeros((C, F), jnp.float32)

    def four(step, carried):
        near, far, state = carried
        base = step * 4
        data = jnp.concatenate([taps_ref[base + k] for k in range(4)], 1)
        out = jnp.dot(weight, data, preferred_element_type=jnp.float32)
        part = lambda tap, k: out[tap * C : (tap + 1) * C, k * F : (k + 1) * F]
        state = finish(state, base - 1, near + part(2, 0))
        state = finish(state, base, far + part(1, 0) + part(2, 1))
        state = finish(state, base + 1, part(0, 0) + part(1, 1) + part(2, 2))
        state = finish(state, base + 2, part(0, 1) + part(1, 2) + part(2, 3))
        return part(0, 2) + part(1, 3), part(0, 3), state

    near, _, state = lax.fori_loop(0, F // 4, four, (zero, zero, state))
    return finish(state, F - 1, near)


def net_kernel(
    info, source, stem_w, first_w, second_w, back_w, sums_w, biases, heads, head_bias,
    map_ref, logit_ref,
    pixels, spread_ref, picked, feats, hidden, grads, edge, acc, arrival,
):
    slot = pl.program_id(0)
    live = info[slot, 0]
    top = info[slot, 1]
    left = info[slot, 2]
    target = info[slot, 3]

    @pl.when(live == 0)
    def _():
        map_ref[...] = jnp.zeros_like(map_ref)
        logit_ref[...] = jnp.zeros_like(logit_ref)

    @pl.when(live != 0)
    def _():
        row0 = pl.multiple_of(top // 16 * 16, 16)
        col0 = pl.multiple_of(left // 128 * 128, 128)
        copy = pltpu.make_async_copy(
            source.at[pl.ds(row0, 528), pl.ds(col0, 640)], pixels, arrival
        )
        copy.start()
        for u in range(9):
            at = lax.broadcasted_iota(jnp.int32, (640, F), 0) - (left - col0)
            want = lanes((640, F)) * 4 + (u - 3)
            hit = (at == want) & (want >= 0) & (want < WIN)
            spread_ref[:, u * F : (u + 1) * F] = jnp.where(hit, 1.0, 0.0).astype(jnp.bfloat16)
        row = lax.broadcasted_iota(jnp.int32, (520, 528), 0) - 3
        shift = jnp.where(
            (lanes((520, 528)) - (top - row0) == row) & (row >= 0) & (row < WIN), 1.0, 0.0
        ).astype(jnp.bfloat16)
        copy.wait()
        moved = jnp.dot(shift, pixels[...], preferred_element_type=jnp.float32)
        picked[...] = jnp.dot(
            moved.astype(jnp.bfloat16), spread_ref[...], preferred_element_type=jnp.float32
        )
        edge[...] = jnp.full_like(edge, LOW)
        stem_bias = biases[0]
        lane0 = lanes((C, F)) == 0

        def stem(step, _):
            slabs = []
            for k in range(2):
                start = pl.multiple_of((step * 2 + k) * 16, 16)
                slab = [
                    picked[pl.ds(start, 24), u * F : (u + 1) * F] for u in range(9)
                ]
                slabs.append(jnp.concatenate(slab, 0))
            data = jnp.concatenate(slabs, 1).astype(jnp.bfloat16)
            out = jnp.dot(stem_w[...], data, preferred_element_type=jnp.float32)
            even, odd = edge[0], edge[1]
            for k in range(2):
                for r in range(4):
                    part = lambda n: out[
                        (r * 4 + n) * C : (r * 4 + n + 1) * C, k * F : (k + 1) * F
                    ]
                    e_high = jnp.maximum(jnp.maximum(even, part(0)), part(2))
                    o_high = jnp.maximum(jnp.maximum(odd, part(1)), part(3))
                    even, odd = part(2), part(3)
                    before = jnp.where(lane0, LOW, pltpu.roll(o_high, 1, 1))
                    high = jnp.maximum(jnp.maximum(e_high, o_high), before)
                    high = jnp.maximum(high + stem_bias, 0.0)
                    put_taps(feats, step * 8 + k * 4 + r, high)
            edge[0] = even
            edge[1] = odd
            return 0

        lax.fori_loop(0, F // 8, stem, 0)

        def after_first(state, row, sums):
            row = jnp.maximum(row, 0)
            put_taps(hidden, row, jnp.maximum(sums + biases[1], 0.0))
            return state

        convolved(feats, first_w, after_first, 0)

        head = jnp.where(lanes((C, F)) == target, heads[...], 0.0)
        column = jnp.sum(head, 1, keepdims=True)
        grad = jnp.broadcast_to(
            (column / float(F * F)).astype(jnp.bfloat16).astype(jnp.float32), (C, F)
        )
        acc[...] = jnp.zeros_like(acc)

        def after_second(state, row, sums):
            keep = jnp.where(row >= 0, 1.0, 0.0)
            row = jnp.maximum(row, 0)
            value = sums + feats[row, C : 2 * C, :].astype(jnp.float32) + biases[2]
            value = jnp.maximum(value, 0.0)
            out = jnp.where(value > 0, grad, 0.0)
            acc[0] += value * keep
            acc[1] += out * keep
            put_taps(grads, row, out)
            return state

        convolved(hidden, second_w, after_second, 0)

        def after_back(state, row, sums):
            keep = jnp.where(row >= 0, 1.0, 0.0)
            row = jnp.maximum(row, 0)
            open_ = hidden[row, C : 2 * C, :].astype(jnp.float32) > 0
            value = jnp.where(open_, sums, 0.0).astype(jnp.bfloat16).astype(jnp.float32)
            acc[2] += value * keep
            acc[3] = jnp.where(row == 0, value, acc[3])
            acc[4] = value
            return state

        convolved(grads, back_w, after_back, 0)

        mean = jnp.sum(acc[0], 1, keepdims=True) / float(F * F)
        logit = jnp.sum(mean * column)
        bias = jnp.sum(jnp.where(lanes((1, F)) == target, head_bias[...], 0.0))
        logit_ref[...] = jnp.full((1, 8, F), logit + bias, jnp.float32)

        whole = acc[2]
        parts = [whole - acc[4], whole, whole - acc[3]]
        weights = jnp.zeros((1, C), jnp.float32)
        lane = lanes((C, F))
        for dy in range(3):
            for dx in range(3):
                drop = {0: F - 1, 1: F, 2: 0}[dx]
                total = jnp.sum(jnp.where(lane == drop, 0.0, parts[dy]), 1, keepdims=True)
                weights += jnp.sum(sums_w[dy * 3 + dx] * total, 0, keepdims=True)
        eye = lax.broadcasted_iota(jnp.int32, (C, C), 0) == lanes((C, C))
        channel = jnp.sum(jnp.where(eye, weights, 0.0), 1, keepdims=True)
        channel = channel + jnp.sum(acc[1], 1, keepdims=True)
        channel = jnp.broadcast_to(channel, (C, F))

        def rows(step, _):
            base = pl.multiple_of(step * 8, 8)
            found = [
                jnp.sum(
                    feats[base + k, C : 2 * C, :].astype(jnp.float32) * channel, 0, keepdims=True
                )
                for k in range(8)
            ]
            map_ref[0, pl.ds(base, 8), :] = jnp.maximum(jnp.concatenate(found, 0), 0.0)
            return 0

        lax.fori_loop(0, F // 8, rows, 0)


def networks(source, info, stem_weight, stem_bias, conv1_weight, conv1_bias, conv2_weight,
             conv2_bias, head_weight, head_bias):
    slots = info.shape[0]
    stem, first, second, back, sums = arranged(stem_weight, conv1_weight, conv2_weight)
    biases = jnp.broadcast_to(
        jnp.stack([stem_bias, conv1_bias, conv2_bias])[:, :, None], (3, C, F)
    )
    heads = jnp.pad(head_weight.astype(jnp.float32), ((0, 0), (0, F - 9)))
    bias_row = jnp.pad(head_bias[None], ((0, 0), (0, F - 9)))
    whole = pl.BlockSpec(memory_space=pltpu.VMEM)
    maps, logits = pl.pallas_call(
        net_kernel,
        grid_spec=pltpu.PrefetchScalarGridSpec(
            num_scalar_prefetch=1,
            grid=(slots,),
            in_specs=[pl.BlockSpec(memory_space=pl.ANY)] + [whole] * 8,
            out_specs=[
                pl.BlockSpec((1, F, F), lambda i, info: (i, 0, 0)),
                pl.BlockSpec((1, 8, F), lambda i, info: (i, 0, 0)),
            ],
            scratch_shapes=[
                pltpu.VMEM((528, 640), jnp.bfloat16),
                pltpu.VMEM((640, 9 * F), jnp.bfloat16),
                pltpu.VMEM((520, 9 * F), jnp.float32),
                pltpu.VMEM((F, 3 * C, F), jnp.bfloat16),
                pltpu.VMEM((F, 3 * C, F), jnp.bfloat16),
                pltpu.VMEM((F, 3 * C, F), jnp.bfloat16),
                pltpu.VMEM((2, C, F), jnp.float32),
                pltpu.VMEM((5, C, F), jnp.float32),
                pltpu.SemaphoreType.DMA,
            ],
        ),
        out_shape=[
            jax.ShapeDtypeStruct((slots, F, F), jnp.float32),
            jax.ShapeDtypeStruct((slots, 8, F), jnp.float32),
        ],
        compiler_params=pltpu.CompilerParams(vmem_limit_bytes=56 << 20),
    )(info, source, stem, first, second, back, sums, biases, heads, bias_row)
    return maps, logits[:, 0, 0]


def blend_kernel(info, maps, out_ref, below):
    size = out_ref.shape[0]
    out_ref[...] = jnp.zeros_like(out_ref)
    below[...] = jnp.zeros_like(below)

    def profile(offset):
        value = (offset - (WIN - 1) / 2.0) * (1.0 / (WIN / 4.0))
        return jnp.exp(-0.5 * value * value)

    def window(number, _):
        top = info[number, 1]
        left = info[number, 2]

        @pl.when(info[number, 0] != 0)
        def _():
            row0 = pl.multiple_of(jnp.clip(top // 8 * 8, 0, size - 520), 8)
            col0 = pl.multiple_of(jnp.clip(left // 128 * 128, 0, size - 640), 128)
            row = lax.broadcasted_iota(jnp.int32, (520, F), 0) + (row0 - top)
            in_row = (row >= 0) & (row < WIN)
            up = jnp.where(in_row & (row // 4 == lanes((520, F))), 1.0, 0.0)
            down = jnp.where(in_row, profile(row.astype(jnp.float32)), 0.0)
            col = lanes((F, 640)) + (col0 - left)
            in_col = (col >= 0) & (col < WIN)
            tap = lax.broadcasted_iota(jnp.int32, (F, 640), 0)
            across = jnp.where(in_col & (col // 4 == tap), 1.0, 0.0).astype(jnp.bfloat16)
            col = lanes((8, 640)) + (col0 - left)
            in_col = (col >= 0) & (col < WIN)
            side = jnp.where(in_col, profile(col.astype(jnp.float32)), 0.0)[0:1]
            tall = jnp.dot(
                up.astype(jnp.bfloat16), maps[number], preferred_element_type=jnp.float32
            ).astype(jnp.bfloat16)
            for k in range(5):
                part = slice(k * F, (k + 1) * F)
                at = (pl.ds(row0, 520), pl.ds(pl.multiple_of(col0 + k * F, F), F))
                weight = down * side[:, part]
                value = jnp.dot(tall, across[:, part], preferred_element_type=jnp.float32)
                out_ref[at] += value * weight
                below[at] += weight
        return 0

    lax.fori_loop(0, info.shape[0], window, 0)
    out_ref[...] = out_ref[...] / jnp.maximum(below[...], 1.0)


def blend(info, maps, size):
    return pl.pallas_call(
        blend_kernel,
        grid_spec=pltpu.PrefetchScalarGridSpec(
            num_scalar_prefetch=1,
            grid=(1,),
            in_specs=[pl.BlockSpec(memory_space=pltpu.VMEM)],
            out_specs=pl.BlockSpec((size, size), lambda i, info: (0, 0)),
            scratch_shapes=[pltpu.VMEM((size, size), jnp.float32)],
        ),
        out_shape=jax.ShapeDtypeStruct((size, size), jnp.float32),
        compiler_params=pltpu.CompilerParams(vmem_limit_bytes=40 << 20),
    )(info, maps)


def moved(shard, down, right):
    rows, cols = lax.axis_size("row"), lax.axis_size("col")
    pairs = [
        (r * cols + c, (r + down) * cols + c + right)
        for r in range(rows)
        for c in range(cols)
        if 0 <= r + down < rows and 0 <= c + right < cols
    ]
    return lax.ppermute(shard, ("row", "col"), pairs)


def local(scan, anchors, targets, *network):
    size = scan.shape[0]
    row_index = lax.axis_index("row")
    col_index = lax.axis_index("col")
    pixels = scan.astype(jnp.bfloat16)
    corners = anchors.reshape(-1, 2)
    live = (corners[:, 0] >= 0).astype(jnp.int32)
    here = jnp.stack([row_index, col_index]) * size
    own = jnp.concatenate(
        [live[:, None], corners - here[None], targets.reshape(-1, 1).astype(jnp.int32)], 1
    )
    ways = ((0, 1), (1, 0), (1, 1))
    reach = [own]
    for down, right in ways:
        info = moved(own, down, right)
        there = (row_index >= down) & (col_index >= right)
        shift = jnp.array([0, -down * size, -right * size, 0], jnp.int32)
        info = info + shift
        hit = there & (info[:, 0] != 0) & (info[:, 1] > -WIN) & (info[:, 2] > -WIN)
        reach.append(jnp.where(hit[:, None], info, 0))
    below = moved(pixels[:WIN], -1, 0)
    right = moved(pixels[:, :WIN], 0, -1)
    corner = moved(pixels[:WIN, :WIN], -1, -1)
    framed = jnp.concatenate(
        [jnp.concatenate([pixels, right], 1), jnp.concatenate([below, corner], 1)], 0
    )
    maps, scores = networks(framed, own, *network)
    maps = maps.astype(jnp.bfloat16)
    every = jnp.concatenate([maps] + [moved(maps, down, right) for down, right in ways], 0)
    saliency = blend(jnp.concatenate(reach, 0), every, size)
    return saliency, scores.reshape(targets.shape)


def solution(mesh):
    placed = (
        P("row", "col"),
        P(None, "row", "col", None),
        P(None, "row", "col"),
    ) + (P(),) * 8
    return jax.shard_map(
        local,
        mesh=mesh,
        in_specs=placed,
        out_specs=(P("row", "col"), P(None, "row", "col")),
        check_vma=False,
    )
```

```python
import jax
import jax.numpy as jnp
from jax import lax
from jax.experimental import pallas as pl
from jax.experimental.pallas import tpu as pltpu
from jax.sharding import PartitionSpec as P

TILE = 1024
WIN = 512
RIM = 512
C = 64
F = 128
SLOTS = 4
BLOCKS = 16
ROWS = 64
LOW = -3.0e38
MESH = pl.DeviceIdType.MESH
WAYS = ((0, 0), (0, 1), (1, 0), (1, 1))


def lanes(shape):
    return lax.broadcasted_iota(jnp.int32, shape, len(shape) - 1)


def frame_kernel(
    scan, own, framed, infos,
    raw, pixels, loads, keeps, up_send, up_recv, left_send, left_recv,
    corner_send, corner_recv, info_send, info_recv,
):
    row, col = lax.axis_index("row"), lax.axis_index("col")
    rows, cols = lax.axis_size("row"), lax.axis_size("col")
    up, down, left, right = row > 0, row < rows - 1, col > 0, col < cols - 1
    chunks = TILE // F
    fetch = [
        pltpu.make_async_copy(scan.at[pl.ds(k * F, F)], raw.at[pl.ds(k * F, F)], loads.at[k])
        for k in range(chunks)
    ]
    for copy in fetch:
        copy.start()
    infos[...] = jnp.full_like(infos, -1)
    infos[0] = own[...]

    barrier = pltpu.get_barrier_semaphore()
    partners = (
        (-1, 0, up), (1, 0, down), (0, -1, left), (0, 1, right),
        (1, 1, down & right), (-1, -1, up & left),
    )
    for by_row, by_col, there in partners:
        @pl.when(there)
        def _():
            pl.semaphore_signal(
                barrier, inc=1, device_id=(row + by_row, col + by_col), device_id_type=MESH
            )
    pl.semaphore_wait(barrier, sum(there.astype(jnp.int32) for _, _, there in partners))

    def remote(source, target, send, recv, by_row, by_col):
        return pltpu.make_async_remote_copy(
            src_ref=source, dst_ref=target, send_sem=send, recv_sem=recv,
            device_id=(row + by_row, col + by_col), device_id_type=MESH,
        )

    def part(k):
        return pl.ds(k * F, F)

    def under(k):
        return pl.ds(TILE + k * F, F)

    ups = [
        remote(pixels.at[part(k)], framed.at[under(k), pl.ds(0, TILE)],
               up_send.at[k], up_recv.at[k], -1, 0)
        for k in range(RIM // F)
    ]
    lefts = [
        remote(pixels.at[part(k), pl.ds(0, RIM)], framed.at[part(k), pl.ds(TILE, RIM)],
               left_send.at[k], left_recv.at[k], 0, -1)
        for k in range(chunks)
    ]
    corners = [
        remote(framed.at[under(k), pl.ds(0, RIM)], framed.at[under(k), pl.ds(TILE, RIM)],
               corner_send.at[k], corner_recv.at[k], 0, -1)
        for k in range(RIM // F)
    ]
    tells = [
        (remote(own, infos.at[1], info_send.at[0], info_recv.at[0], 0, 1), right, left),
        (remote(own, infos.at[2], info_send.at[1], info_recv.at[1], 1, 0), down, up),
        (remote(own, infos.at[3], info_send.at[2], info_recv.at[2], 1, 1), down & right, up & left),
    ]
    kept = [
        pltpu.make_async_copy(pixels.at[part(k)], framed.at[part(k), pl.ds(0, TILE)], keeps.at[k])
        for k in range(chunks)
    ]
    for k in range(chunks):
        fetch[k].wait()
        pixels[k * F : (k + 1) * F, :] = raw[k * F : (k + 1) * F, :].astype(jnp.bfloat16)
        if k < len(ups):
            pl.when(up)(ups[k].start)
        pl.when(left)(lefts[k].start)
        kept[k].start()
    for tell, goes, _ in tells:
        pl.when(goes)(tell.start)
    for k in range(len(ups)):
        pl.when(down)(ups[k].wait_recv)
        pl.when(down & left)(corners[k].start)
    for tell, goes, comes in tells:
        pl.when(goes)(tell.wait_send)
        pl.when(comes)(tell.wait_recv)
    for k in range(chunks):
        kept[k].wait()
        pl.when(left)(lefts[k].wait_send)
        pl.when(right)(lefts[k].wait_recv)
        if k < len(ups):
            pl.when(up)(ups[k].wait_send)
            pl.when(down & left)(corners[k].wait_send)
            pl.when(down & right)(corners[k].wait_recv)


def frame(scan, own):
    chunks, rim = TILE // F, RIM // F
    sems = [chunks, chunks, rim, rim, chunks, chunks, rim, rim, 3, 3]
    return pl.pallas_call(
        frame_kernel,
        out_shape=[
            jax.ShapeDtypeStruct((TILE + RIM, TILE + RIM), jnp.bfloat16),
            jax.ShapeDtypeStruct((4, 8, F), jnp.int32),
        ],
        in_specs=[pl.BlockSpec(memory_space=pl.ANY), pl.BlockSpec(memory_space=pltpu.VMEM)],
        out_specs=[pl.BlockSpec(memory_space=pl.ANY), pl.BlockSpec(memory_space=pltpu.VMEM)],
        scratch_shapes=[
            pltpu.VMEM((TILE, TILE), jnp.float32),
            pltpu.VMEM((TILE, TILE), jnp.bfloat16),
        ] + [pltpu.SemaphoreType.DMA((n,)) for n in sems],
        compiler_params=pltpu.CompilerParams(
            collective_id=0, has_side_effects=True, vmem_limit_bytes=16 << 20
        ),
    )(scan, own)


def put_taps(ref, row, value):
    value = value.astype(jnp.bfloat16)
    lane = lanes((C, F))
    none = jnp.zeros((), jnp.bfloat16)
    ref[row, 0:C, :] = jnp.where(lane == 0, none, pltpu.roll(value, 1, 1))
    ref[row, C : 2 * C, :] = value
    ref[row, 2 * C : 3 * C, :] = jnp.where(lane == F - 1, none, pltpu.roll(value, F - 1, 1))


def convolved(taps_ref, weight_ref, finish):
    weight = weight_ref[...]
    zero = jnp.zeros((C, F), jnp.float32)

    def several(step, carried):
        near, far = carried
        base = step * ROWS
        data = jnp.concatenate([taps_ref[base + k] for k in range(ROWS)], 1)
        out = jnp.dot(weight, data, preferred_element_type=jnp.float32)
        part = lambda tap, k: out[tap * C : (tap + 1) * C, k * F : (k + 1) * F]
        finish(base - 1, near + part(2, 0))
        finish(base, far + part(1, 0) + part(2, 1))
        for k in range(1, ROWS - 1):
            finish(base + k, part(0, k - 1) + part(1, k) + part(2, k + 1))
        return part(0, ROWS - 2) + part(1, ROWS - 1), part(0, ROWS - 1)

    near, _ = lax.fori_loop(0, F // ROWS, several, (zero, zero))
    finish(F - 1, near)


def arrange(stem_raw, first_raw, second_raw, biases_raw, stem_w, first_w, second_w, back_w, biases):
    turned = stem_raw[...].astype(jnp.float32).T.astype(jnp.bfloat16)
    tap = lax.broadcasted_iota(jnp.int32, (49, 216), 0)
    tap_row, tap_col = tap // 7, tap % 7
    place_col, place_row = lanes((49, 216)) // 24, lanes((49, 216)) % 24
    for r in range(8):
        for q in range(2):
            hit = (place_row == 2 * r + tap_row) & (place_col == 2 * q + tap_col)
            hit = jnp.where(hit, 1.0, 0.0).astype(jnp.bfloat16)
            at = (r * 2 + q) * C
            stem_w[at : at + C, :] = jnp.dot(
                turned, hit, preferred_element_type=jnp.float32
            ).astype(jnp.bfloat16)
    for raw, laid in ((first_raw, first_w), (second_raw, second_w)):
        for dy in range(3):
            block = raw[dy * 3 : dy * 3 + 3].reshape(3 * C, C).astype(jnp.float32)
            laid[dy * C : (dy + 1) * C, :] = block.T.astype(jnp.bfloat16)
    for dy in range(3):
        blocks = [second_raw[(2 - dy) * 3 + (2 - dx)] for dx in range(3)]
        back_w[dy * C : (dy + 1) * C, :] = jnp.concatenate(blocks, 1)
    eye = lax.broadcasted_iota(jnp.int32, (C, C), 0) == lanes((C, C))
    for k in range(3):
        upright = jnp.sum(jnp.where(eye, biases_raw[k : k + 1, :], 0.0), 1, keepdims=True)
        biases[k] = jnp.broadcast_to(upright, (C, F))


def net_kernel(
    infos, source, stem_raw, first_raw, second_raw, biases_raw, heads, head_bias,
    map_ref, logit_ref,
    stem_w, first_w, second_w, back_w, biases,
    pixels, spread_ref, picked, feats, hidden, grads, acc, order, arrival,
):
    count = jnp.int32(0)
    for slot in range(SLOTS):
        live = infos[0, slot, 0] >= 0

        @pl.when(live)
        def _():
            order[count] = slot

        count = count + live.astype(jnp.int32)

    def place(number):
        slot = order[number]
        return slot, infos[0, slot, 0] % TILE, infos[0, slot, 1] % TILE, infos[0, slot, 2]

    def fetch(number):
        _, top, left, _ = place(number)
        row0 = pl.multiple_of(top // 16 * 16, 16)
        col0 = pl.multiple_of(left // F * F, F)
        here = number % 2
        return pltpu.make_async_copy(
            source.at[pl.ds(row0, 528), pl.ds(col0, 640)], pixels.at[here], arrival.at[here]
        )

    @pl.when(count > 0)
    def _():
        fetch(0).start()

    arrange(
        stem_raw, first_raw, second_raw, biases_raw, stem_w, first_w, second_w, back_w, biases
    )
    map_ref[...] = jnp.zeros_like(map_ref)
    logit_ref[...] = jnp.zeros_like(logit_ref)

    def window(number, _):
        slot, top, left, target = place(number)

        @pl.when(number + 1 < count)
        def _():
            fetch(number + 1).start()

        over = left % F
        for u in range(9):
            at = lax.broadcasted_iota(jnp.int32, (640, F), 0) - over
            want = lanes((640, F)) * 4 + (u - 3)
            hit = (at == want) & (want >= 0) & (want < WIN)
            spread_ref[:, u * F : (u + 1) * F] = jnp.where(hit, 1.0, 0.0).astype(jnp.bfloat16)
        below = top % 16
        row = lax.broadcasted_iota(jnp.int32, (520, 528), 0) - 3
        shift = jnp.where(
            (lanes((520, 528)) - below == row) & (row >= 0) & (row < WIN), 1.0, 0.0
        ).astype(jnp.bfloat16)
        fetch(number).wait()
        row = lax.broadcasted_iota(jnp.int32, (528, 640), 0) - below
        column = lanes((528, 640)) - over
        inside = (row >= 0) & (row < WIN) & (column >= 0) & (column < WIN)
        found = jnp.where(inside, pixels[number % 2].astype(jnp.float32), 0.0)
        moved = jnp.dot(shift, found.astype(jnp.bfloat16), preferred_element_type=jnp.float32)
        picked[...] = jnp.dot(
            moved.astype(jnp.bfloat16), spread_ref[...], preferred_element_type=jnp.float32
        )
        stem_bias = biases[0]
        lane0 = lanes((C, F)) == 0
        none = jnp.zeros((), jnp.bfloat16)

        def stem(step, carried):
            even, odd = carried
            slabs = []
            for k in range(BLOCKS):
                start = pl.multiple_of((step * BLOCKS + k) * 16, 16)
                slab = [picked[pl.ds(start, 24), u * F : (u + 1) * F] for u in range(9)]
                slabs.append(jnp.concatenate(slab, 0))
            data = jnp.concatenate(slabs, 1).astype(jnp.bfloat16)
            out = jnp.dot(stem_w[...], data, preferred_element_type=jnp.float32)
            for k in range(BLOCKS):
                for r in range(4):
                    part = lambda n: out[
                        (r * 4 + n) * C : (r * 4 + n + 1) * C, k * F : (k + 1) * F
                    ]
                    e_high = jnp.maximum(jnp.maximum(even, part(0)), part(2))
                    o_high = jnp.maximum(jnp.maximum(odd, part(1)), part(3))
                    even, odd = part(2), part(3)
                    high = jnp.maximum(e_high, o_high) + stem_bias
                    high = jnp.maximum(high, 0.0).astype(jnp.bfloat16)
                    side = jnp.maximum(o_high + stem_bias, 0.0).astype(jnp.bfloat16)
                    before = jnp.where(lane0, none, pltpu.roll(side, 1, 1))
                    put_taps(feats, (step * BLOCKS + k) * 4 + r, jnp.maximum(high, before))
            return even, odd

        low = jnp.full((C, F), LOW, jnp.float32)
        lax.fori_loop(0, F // 4 // BLOCKS, stem, (low, low))

        def after_first(row, sums):
            put_taps(hidden, jnp.maximum(row, 0), jnp.maximum(sums + biases[1], 0.0))

        convolved(feats, first_w, after_first)

        head = jnp.where(lanes((C, 9)) == target, heads[...].astype(jnp.float32), 0.0)
        column = jnp.sum(head, 1, keepdims=True)
        grad = jnp.broadcast_to(
            (column / float(F * F)).astype(jnp.bfloat16).astype(jnp.float32), (C, F)
        )
        acc[...] = jnp.zeros_like(acc)

        def after_second(row, sums):
            keep = jnp.where(row >= 0, 1.0, 0.0)
            row = jnp.maximum(row, 0)
            value = sums + feats[row, C : 2 * C, :].astype(jnp.float32) + biases[2]
            value = jnp.maximum(value, 0.0)
            out = jnp.where(value > 0, grad, 0.0)
            acc[0] += value * keep
            acc[1] += out * keep
            put_taps(grads, row, out)

        convolved(hidden, second_w, after_second)

        def after_back(row, sums):
            keep = jnp.where(row >= 0, 1.0, 0.0)
            row = jnp.maximum(row, 0)
            open_ = hidden[row, C : 2 * C, :].astype(jnp.float32) > 0
            value = jnp.where(open_, sums, 0.0).astype(jnp.bfloat16).astype(jnp.float32)
            acc[2] += value * keep
            acc[3] = jnp.where(row == 0, value, acc[3])
            acc[4] = value

        convolved(grads, back_w, after_back)

        mean = jnp.sum(acc[0], 1, keepdims=True) / float(F * F)
        logit = jnp.sum(mean * column)
        bias = jnp.sum(jnp.where(lanes((1, 9)) == target, head_bias[...], 0.0))
        logit_ref[slot] = jnp.full((8, F), logit + bias, jnp.float32)

        whole = acc[2]
        parts = [whole - acc[4], whole, whole - acc[3]]
        lane = lanes((C, F))
        eye = lax.broadcasted_iota(jnp.int32, (C, C), 0) == lanes((C, C))
        channel = jnp.sum(acc[1], 1, keepdims=True)
        for dy in range(3):
            for dx in range(3):
                drop = {0: F - 1, 1: F, 2: 0}[dx]
                total = jnp.sum(jnp.where(lane == drop, 0.0, parts[dy]), 1, keepdims=True)
                flat = jnp.sum(jnp.where(eye, total, 0.0), 0, keepdims=True)
                weight = first_raw[(2 - dy) * 3 + (2 - dx)].astype(jnp.float32)
                channel = channel + jnp.sum(weight * flat, 1, keepdims=True)
        channel = jnp.broadcast_to(channel, (C, F))

        def rows(step, _):
            base = pl.multiple_of(step * 16, 16)
            found = [
                jnp.sum(
                    feats[base + k, C : 2 * C, :].astype(jnp.float32) * channel, 0, keepdims=True
                )
                for k in range(16)
            ]
            found = jnp.maximum(jnp.concatenate(found, 0), 0.0)
            map_ref[slot, pl.ds(base, 16), :] = found.astype(jnp.bfloat16)
            return 0

        lax.fori_loop(0, F // 16, rows, 0)
        return 0

    lax.fori_loop(0, count, window, 0)


def networks(infos, framed, stem_weight, stem_bias, conv1_weight, conv1_bias, conv2_weight,
             conv2_bias, head_weight, head_bias):
    biases = jnp.stack([stem_bias, conv1_bias, conv2_bias])
    whole = pl.BlockSpec(memory_space=pltpu.VMEM)
    maps, logits = pl.pallas_call(
        net_kernel,
        in_specs=[pl.BlockSpec(memory_space=pltpu.SMEM), pl.BlockSpec(memory_space=pl.ANY)]
        + [whole] * 6,
        out_specs=[whole, whole],
        scratch_shapes=[
            pltpu.VMEM((16 * C, 216), jnp.bfloat16),
            pltpu.VMEM((3 * C, 3 * C), jnp.bfloat16),
            pltpu.VMEM((3 * C, 3 * C), jnp.bfloat16),
            pltpu.VMEM((3 * C, 3 * C), jnp.bfloat16),
            pltpu.VMEM((3, C, F), jnp.float32),
            pltpu.VMEM((2, 528, 640), jnp.bfloat16),
            pltpu.VMEM((640, 9 * F), jnp.bfloat16),
            pltpu.VMEM((520, 9 * F), jnp.float32),
            pltpu.VMEM((F, 3 * C, F), jnp.bfloat16),
            pltpu.VMEM((F, 3 * C, F), jnp.bfloat16),
            pltpu.VMEM((F, 3 * C, F), jnp.bfloat16),
            pltpu.VMEM((5, C, F), jnp.float32),
            pltpu.SMEM((SLOTS,), jnp.int32),
            pltpu.SemaphoreType.DMA((2,)),
        ],
        out_shape=[
            jax.ShapeDtypeStruct((SLOTS, F, F), jnp.bfloat16),
            jax.ShapeDtypeStruct((SLOTS, 8, F), jnp.float32),
        ],
        compiler_params=pltpu.CompilerParams(vmem_limit_bytes=58 << 20),
    )(
        infos, framed, stem_weight.reshape(49, C), conv1_weight.reshape(9, C, C),
        conv2_weight.reshape(9, C, C), biases, head_weight, head_bias.reshape(1, 9),
    )
    return maps, logits[:, 0, 0]


def blend_kernel(infos, maps, out_ref, total):
    out_ref[...] = jnp.zeros_like(out_ref)
    total[...] = jnp.zeros_like(total)

    def profile(offset):
        value = (offset - (WIN - 1) / 2.0) * (1.0 / (WIN / 4.0))
        return jnp.exp(-0.5 * value * value)

    def window(number, _):
        way, slot = number // SLOTS, number % SLOTS
        corner = infos[way, slot, 0]
        top = corner % TILE - way // 2 * TILE
        left = infos[way, slot, 1] % TILE - way % 2 * TILE

        @pl.when((corner >= 0) & (top > -WIN) & (left > -WIN))
        def _():
            row0 = pl.multiple_of(jnp.clip(top // 8 * 8, 0, TILE - 520), 8)
            col0 = pl.multiple_of(jnp.clip(left // F * F, 0, TILE - 640), F)
            row = lax.broadcasted_iota(jnp.int32, (520, F), 0) + (row0 - top)
            in_row = (row >= 0) & (row < WIN)
            up = jnp.where(in_row & (row // 4 == lanes((520, F))), 1.0, 0.0)
            down = jnp.where(in_row, profile(row.astype(jnp.float32)), 0.0)
            col = lanes((F, 640)) + (col0 - left)
            in_col = (col >= 0) & (col < WIN)
            tap = lax.broadcasted_iota(jnp.int32, (F, 640), 0)
            across = jnp.where(in_col & (col // 4 == tap), 1.0, 0.0).astype(jnp.bfloat16)
            col = lanes((8, 640)) + (col0 - left)
            in_col = (col >= 0) & (col < WIN)
            side = jnp.where(in_col, profile(col.astype(jnp.float32)), 0.0)[0:1]
            tall = jnp.dot(
                up.astype(jnp.bfloat16), maps[number], preferred_element_type=jnp.float32
            ).astype(jnp.bfloat16)
            for k in range(5):
                part = slice(k * F, (k + 1) * F)
                at = (pl.ds(row0, 520), pl.ds(pl.multiple_of(col0 + k * F, F), F))
                weight = down * side[:, part]
                value = jnp.dot(tall, across[:, part], preferred_element_type=jnp.float32)
                out_ref[at] += value * weight
                total[at] += weight
        return 0

    lax.fori_loop(0, 4 * SLOTS, window, 0)
    out_ref[...] = out_ref[...] / jnp.maximum(total[...], 1.0)


def blend(infos, maps):
    return pl.pallas_call(
        blend_kernel,
        in_specs=[
            pl.BlockSpec(memory_space=pltpu.SMEM),
            pl.BlockSpec(memory_space=pltpu.VMEM),
        ],
        out_specs=pl.BlockSpec(memory_space=pltpu.VMEM),
        scratch_shapes=[pltpu.VMEM((TILE, TILE), jnp.float32)],
        out_shape=jax.ShapeDtypeStruct((TILE, TILE), jnp.float32),
        compiler_params=pltpu.CompilerParams(vmem_limit_bytes=40 << 20),
    )(infos, maps)


def moved(shard, down, right):
    rows, cols = lax.axis_size("row"), lax.axis_size("col")
    pairs = [
        (r * cols + c, (r + down) * cols + c + right)
        for r in range(rows)
        for c in range(cols)
        if 0 <= r + down < rows and 0 <= c + right < cols
    ]
    return lax.ppermute(shard, ("row", "col"), pairs)


def local(scan, anchors, targets, *network):
    own = jnp.concatenate([anchors.reshape(SLOTS, 2), targets.reshape(SLOTS, 1)], 1)
    own = jnp.pad(own, ((0, 8 - SLOTS), (0, F - 3)), constant_values=-1)
    framed, infos = frame(scan, own)
    maps, scores = networks(infos, framed, *network)
    every = jnp.concatenate([maps] + [moved(maps, *way) for way in WAYS[1:]], 0)
    saliency = blend(infos, every)
    return saliency, scores.reshape(targets.shape)


def solution(mesh):
    placed = (
        P("row", "col"),
        P(None, "row", "col", None),
        P(None, "row", "col"),
    ) + (P(),) * 8
    return jax.shard_map(
        local,
        mesh=mesh,
        in_specs=placed,
        out_specs=(P("row", "col"), P(None, "row", "col")),
        check_vma=False,
    )
```

```python
import jax
import jax.numpy as jnp
from jax import lax
from jax.experimental import pallas as pl
from jax.experimental.pallas import tpu as pltpu
from jax.sharding import PartitionSpec as P

TILE = 1024
WIN = 512
RIM = 512
C = 64
F = 128
SLOTS = 4
BLOCKS = 32
ROWS = 128
LOW = -3.0e38
MESH = pl.DeviceIdType.MESH
WAYS = ((0, 0), (0, 1), (1, 0), (1, 1))


def lanes(shape):
    return lax.broadcasted_iota(jnp.int32, shape, len(shape) - 1)


def frame_kernel(
    scan, own, framed, infos,
    raw, pixels, loads, keeps, up_send, up_recv, left_send, left_recv,
    corner_send, corner_recv, info_send, info_recv,
):
    row, col = lax.axis_index("row"), lax.axis_index("col")
    rows, cols = lax.axis_size("row"), lax.axis_size("col")
    up, down, left, right = row > 0, row < rows - 1, col > 0, col < cols - 1
    chunks = TILE // F
    fetch = [
        pltpu.make_async_copy(scan.at[pl.ds(k * F, F)], raw.at[pl.ds(k * F, F)], loads.at[k])
        for k in range(chunks)
    ]
    for copy in fetch:
        copy.start()
    infos[...] = jnp.full_like(infos, -1)
    infos[0] = own[...]

    barrier = pltpu.get_barrier_semaphore()
    partners = (
        (-1, 0, up), (1, 0, down), (0, -1, left), (0, 1, right),
        (1, 1, down & right), (-1, -1, up & left),
    )
    for by_row, by_col, there in partners:
        @pl.when(there)
        def _():
            pl.semaphore_signal(
                barrier, inc=1, device_id=(row + by_row, col + by_col), device_id_type=MESH
            )
    pl.semaphore_wait(barrier, sum(there.astype(jnp.int32) for _, _, there in partners))

    def remote(source, target, send, recv, by_row, by_col):
        return pltpu.make_async_remote_copy(
            src_ref=source, dst_ref=target, send_sem=send, recv_sem=recv,
            device_id=(row + by_row, col + by_col), device_id_type=MESH,
        )

    def part(k):
        return pl.ds(k * F, F)

    def under(k):
        return pl.ds(TILE + k * F, F)

    ups = [
        remote(pixels.at[part(k)], framed.at[under(k), pl.ds(0, TILE)],
               up_send.at[k], up_recv.at[k], -1, 0)
        for k in range(RIM // F)
    ]
    lefts = [
        remote(pixels.at[part(k), pl.ds(0, RIM)], framed.at[part(k), pl.ds(TILE, RIM)],
               left_send.at[k], left_recv.at[k], 0, -1)
        for k in range(chunks)
    ]
    corners = [
        remote(framed.at[under(k), pl.ds(0, RIM)], framed.at[under(k), pl.ds(TILE, RIM)],
               corner_send.at[k], corner_recv.at[k], 0, -1)
        for k in range(RIM // F)
    ]
    tells = [
        (remote(own, infos.at[1], info_send.at[0], info_recv.at[0], 0, 1), right, left),
        (remote(own, infos.at[2], info_send.at[1], info_recv.at[1], 1, 0), down, up),
        (remote(own, infos.at[3], info_send.at[2], info_recv.at[2], 1, 1), down & right, up & left),
    ]
    kept = [
        pltpu.make_async_copy(pixels.at[part(k)], framed.at[part(k), pl.ds(0, TILE)], keeps.at[k])
        for k in range(chunks)
    ]
    for k in range(chunks):
        fetch[k].wait()
        pixels[k * F : (k + 1) * F, :] = raw[k * F : (k + 1) * F, :].astype(jnp.bfloat16)
        if k < len(ups):
            pl.when(up)(ups[k].start)
        pl.when(left)(lefts[k].start)
        kept[k].start()
    for tell, goes, _ in tells:
        pl.when(goes)(tell.start)
    for k in range(len(ups)):
        pl.when(down)(ups[k].wait_recv)
        pl.when(down & left)(corners[k].start)
    for tell, goes, comes in tells:
        pl.when(goes)(tell.wait_send)
        pl.when(comes)(tell.wait_recv)
    for k in range(chunks):
        kept[k].wait()
        pl.when(left)(lefts[k].wait_send)
        pl.when(right)(lefts[k].wait_recv)
        if k < len(ups):
            pl.when(up)(ups[k].wait_send)
            pl.when(down & left)(corners[k].wait_send)
            pl.when(down & right)(corners[k].wait_recv)


def frame(scan, own):
    chunks, rim = TILE // F, RIM // F
    sems = [chunks, chunks, rim, rim, chunks, chunks, rim, rim, 3, 3]
    return pl.pallas_call(
        frame_kernel,
        out_shape=[
            jax.ShapeDtypeStruct((TILE + RIM, TILE + RIM), jnp.bfloat16),
            jax.ShapeDtypeStruct((4, 8, F), jnp.int32),
        ],
        in_specs=[pl.BlockSpec(memory_space=pltpu.HBM), pl.BlockSpec(memory_space=pltpu.VMEM)],
        out_specs=[pl.BlockSpec(memory_space=pltpu.HBM), pl.BlockSpec(memory_space=pltpu.VMEM)],
        scratch_shapes=[
            pltpu.VMEM((TILE, TILE), jnp.float32),
            pltpu.VMEM((TILE, TILE), jnp.bfloat16),
        ] + [pltpu.SemaphoreType.DMA((n,)) for n in sems],
        compiler_params=pltpu.CompilerParams(
            collective_id=0, has_side_effects=True, vmem_limit_bytes=60 << 20
        ),
    )(scan, own)


def put_taps(ref, row, value):
    value = value.astype(jnp.bfloat16)
    lane = lanes((C, F))
    none = jnp.zeros((), jnp.bfloat16)
    ref[row, 0:C, :] = jnp.where(lane == 0, none, pltpu.roll(value, 1, 1))
    ref[row, C : 2 * C, :] = value
    ref[row, 2 * C : 3 * C, :] = jnp.where(lane == F - 1, none, pltpu.roll(value, F - 1, 1))


def convolved(taps_ref, weight_ref, finish):
    weight = weight_ref[...]
    zero = jnp.zeros((C, F), jnp.float32)

    def several(step, carried):
        near, far = carried
        base = step * ROWS
        data = jnp.concatenate([taps_ref[base + k] for k in range(ROWS)], 1)
        out = jnp.dot(weight, data, preferred_element_type=jnp.float32)
        part = lambda tap, k: out[tap * C : (tap + 1) * C, k * F : (k + 1) * F]
        finish(base - 1, near + part(2, 0))
        finish(base, far + part(1, 0) + part(2, 1))
        for k in range(1, ROWS - 1):
            finish(base + k, part(0, k - 1) + part(1, k) + part(2, k + 1))
        return part(0, ROWS - 2) + part(1, ROWS - 1), part(0, ROWS - 1)

    near, _ = lax.fori_loop(0, F // ROWS, several, (zero, zero))
    finish(F - 1, near)


def arrange(stem_raw, first_raw, second_raw, biases_raw, stem_w, first_w, second_w, back_w, biases):
    taps = [stem_raw[k // 7, k % 7].astype(jnp.float32) for k in range(49)]
    turned = jnp.concatenate(taps, 0).T.astype(jnp.bfloat16)
    tap = lax.broadcasted_iota(jnp.int32, (49, 216), 0)
    tap_row, tap_col = tap // 7, tap % 7
    place_col, place_row = lanes((49, 216)) // 24, lanes((49, 216)) % 24
    for r in range(8):
        for q in range(2):
            hit = (place_row == 2 * r + tap_row) & (place_col == 2 * q + tap_col)
            hit = jnp.where(hit, 1.0, 0.0).astype(jnp.bfloat16)
            at = (r * 2 + q) * C
            stem_w[at : at + C, :] = jnp.dot(
                turned, hit, preferred_element_type=jnp.float32
            ).astype(jnp.bfloat16)
    for raw, laid in ((first_raw, first_w), (second_raw, second_w)):
        for dy in range(3):
            block = raw[dy * 3 : dy * 3 + 3].reshape(3 * C, C).astype(jnp.float32)
            laid[dy * C : (dy + 1) * C, :] = block.T.astype(jnp.bfloat16)
    for dy in range(3):
        blocks = [second_raw[(2 - dy) * 3 + (2 - dx)] for dx in range(3)]
        back_w[dy * C : (dy + 1) * C, :] = jnp.concatenate(blocks, 1)
    eye = lax.broadcasted_iota(jnp.int32, (C, C), 0) == lanes((C, C))
    for k in range(3):
        upright = jnp.sum(jnp.where(eye, biases_raw[k : k + 1, :], 0.0), 1, keepdims=True)
        biases[k] = jnp.broadcast_to(upright, (C, F))


def net_kernel(
    infos, source, stem_raw, first_raw, second_raw, biases_raw, heads, head_bias,
    map_ref, logit_ref,
    stem_w, first_w, second_w, back_w, biases,
    pixels, spread_ref, picked, feats, hidden, grads, acc, order, arrival,
):
    count = jnp.int32(0)
    for slot in range(SLOTS):
        live = infos[0, slot, 0] >= 0

        @pl.when(live)
        def _():
            order[count] = slot

        count = count + live.astype(jnp.int32)

    def place(number):
        slot = order[number]
        return slot, infos[0, slot, 0] % TILE, infos[0, slot, 1] % TILE, infos[0, slot, 2]

    def fetch(number):
        _, top, left, _ = place(number)
        row0 = pl.multiple_of(top // 16 * 16, 16)
        col0 = pl.multiple_of(left // F * F, F)
        here = number % 2
        return pltpu.make_async_copy(
            source.at[pl.ds(row0, 528), pl.ds(col0, 640)], pixels.at[here], arrival.at[here]
        )

    @pl.when(count > 0)
    def _():
        fetch(0).start()

    arrange(
        stem_raw, first_raw, second_raw, biases_raw, stem_w, first_w, second_w, back_w, biases
    )
    map_ref[...] = jnp.zeros_like(map_ref)
    for slot in range(SLOTS):
        logit_ref[slot] = jnp.float32(0.0)

    def window(number, _):
        slot, top, left, target = place(number)

        @pl.when(number + 1 < count)
        def _():
            fetch(number + 1).start()

        over = left % F
        for u in range(9):
            at = lax.broadcasted_iota(jnp.int32, (640, F), 0) - over
            want = lanes((640, F)) * 4 + (u - 3)
            hit = (at == want) & (want >= 0) & (want < WIN)
            spread_ref[:, u * F : (u + 1) * F] = jnp.where(hit, 1.0, 0.0).astype(jnp.bfloat16)
        below = top % 16
        row = lax.broadcasted_iota(jnp.int32, (520, 528), 0) - 3
        shift = jnp.where(
            (lanes((520, 528)) - below == row) & (row >= 0) & (row < WIN), 1.0, 0.0
        ).astype(jnp.bfloat16)
        fetch(number).wait()
        row = lax.broadcasted_iota(jnp.int32, (528, 640), 0) - below
        column = lanes((528, 640)) - over
        inside = (row >= 0) & (row < WIN) & (column >= 0) & (column < WIN)
        found = jnp.where(inside, pixels[number % 2].astype(jnp.float32), 0.0)
        moved = jnp.dot(shift, found.astype(jnp.bfloat16), preferred_element_type=jnp.float32)
        picked[...] = jnp.dot(
            moved.astype(jnp.bfloat16), spread_ref[...], preferred_element_type=jnp.float32
        )
        stem_bias = biases[0]
        lane0 = lanes((C, F)) == 0
        none = jnp.zeros((), jnp.bfloat16)

        def stem(step, carried):
            even, odd = carried
            slabs = []
            for k in range(BLOCKS):
                start = pl.multiple_of((step * BLOCKS + k) * 16, 16)
                slab = [picked[pl.ds(start, 24), u * F : (u + 1) * F] for u in range(9)]
                slabs.append(jnp.concatenate(slab, 0))
            data = jnp.concatenate(slabs, 1).astype(jnp.bfloat16)
            out = jnp.dot(stem_w[...], data, preferred_element_type=jnp.float32)
            for k in range(BLOCKS):
                for r in range(4):
                    part = lambda n: out[
                        (r * 4 + n) * C : (r * 4 + n + 1) * C, k * F : (k + 1) * F
                    ]
                    e_high = jnp.maximum(jnp.maximum(even, part(0)), part(2))
                    o_high = jnp.maximum(jnp.maximum(odd, part(1)), part(3))
                    even, odd = part(2), part(3)
                    high = jnp.maximum(e_high, o_high) + stem_bias
                    high = jnp.maximum(high, 0.0).astype(jnp.bfloat16)
                    side = jnp.maximum(o_high + stem_bias, 0.0).astype(jnp.bfloat16)
                    before = jnp.where(lane0, none, pltpu.roll(side, 1, 1))
                    put_taps(feats, (step * BLOCKS + k) * 4 + r, jnp.maximum(high, before))
            return even, odd

        low = jnp.full((C, F), LOW, jnp.float32)
        lax.fori_loop(0, F // 4 // BLOCKS, stem, (low, low))

        def after_first(row, sums):
            put_taps(hidden, jnp.maximum(row, 0), jnp.maximum(sums + biases[1], 0.0))

        convolved(feats, first_w, after_first)

        eye = lax.broadcasted_iota(jnp.int32, (C, C), 0) == lanes((C, C))
        wanted = lax.broadcasted_iota(jnp.int32, (9, C), 0) == target
        head = jnp.where(wanted, heads[...].astype(jnp.float32), 0.0)
        head = jnp.sum(head, 0, keepdims=True)
        column = jnp.sum(jnp.where(eye, head, 0.0), 1, keepdims=True)
        grad = jnp.broadcast_to(
            (column / float(F * F)).astype(jnp.bfloat16).astype(jnp.float32), (C, F)
        )
        acc[...] = jnp.zeros_like(acc)

        def after_second(row, sums):
            keep = jnp.where(row >= 0, 1.0, 0.0)
            row = jnp.maximum(row, 0)
            value = sums + feats[row, C : 2 * C, :].astype(jnp.float32) + biases[2]
            value = jnp.maximum(value, 0.0)
            out = jnp.where(value > 0, grad, 0.0)
            acc[0] += value * keep
            acc[1] += out * keep
            put_taps(grads, row, out)

        convolved(hidden, second_w, after_second)

        def after_back(row, sums):
            keep = jnp.where(row >= 0, 1.0, 0.0)
            row = jnp.maximum(row, 0)
            open_ = hidden[row, C : 2 * C, :].astype(jnp.float32) > 0
            value = jnp.where(open_, sums, 0.0).astype(jnp.bfloat16).astype(jnp.float32)
            acc[2] += value * keep
            acc[3] = jnp.where(row == 0, value, acc[3])
            acc[4] = value

        convolved(grads, back_w, after_back)

        mean = jnp.sum(acc[0], 1, keepdims=True) / float(F * F)
        logit = jnp.sum(mean * column)
        bias = jnp.sum(jnp.where(lanes((1, 9)) == target, head_bias[...], 0.0))
        logit_ref[slot] = logit + bias

        whole = acc[2]
        parts = [whole - acc[4], whole, whole - acc[3]]
        lane = lanes((C, F))
        channel = jnp.sum(acc[1], 1, keepdims=True)
        for dy in range(3):
            for dx in range(3):
                drop = {0: F - 1, 1: F, 2: 0}[dx]
                total = jnp.sum(jnp.where(lane == drop, 0.0, parts[dy]), 1, keepdims=True)
                flat = jnp.sum(jnp.where(eye, total, 0.0), 0, keepdims=True)
                weight = first_raw[(2 - dy) * 3 + (2 - dx)].astype(jnp.float32)
                channel = channel + jnp.sum(weight * flat, 1, keepdims=True)
        channel = jnp.broadcast_to(channel, (C, F))

        def rows(step, _):
            base = pl.multiple_of(step * 16, 16)
            found = [
                jnp.sum(
                    feats[base + k, C : 2 * C, :].astype(jnp.float32) * channel, 0, keepdims=True
                )
                for k in range(16)
            ]
            found = jnp.maximum(jnp.concatenate(found, 0), 0.0)
            map_ref[slot, pl.ds(base, 16), :] = found.astype(jnp.bfloat16)
            return 0

        lax.fori_loop(0, F // 16, rows, 0)
        return 0

    lax.fori_loop(0, count, window, 0)


def networks(infos, framed, stem_weight, stem_bias, conv1_weight, conv1_bias, conv2_weight,
             conv2_bias, head_weight, head_bias):
    biases = jnp.stack([stem_bias, conv1_bias, conv2_bias])
    whole = pl.BlockSpec(memory_space=pltpu.VMEM)
    maps, logits = pl.pallas_call(
        net_kernel,
        in_specs=[pl.BlockSpec(memory_space=pltpu.SMEM), pl.BlockSpec(memory_space=pltpu.HBM)]
        + [whole] * 6,
        out_specs=[whole, pl.BlockSpec(memory_space=pltpu.SMEM)],
        scratch_shapes=[
            pltpu.VMEM((16 * C, 216), jnp.bfloat16),
            pltpu.VMEM((3 * C, 3 * C), jnp.bfloat16),
            pltpu.VMEM((3 * C, 3 * C), jnp.bfloat16),
            pltpu.VMEM((3 * C, 3 * C), jnp.bfloat16),
            pltpu.VMEM((3, C, F), jnp.float32),
            pltpu.VMEM((2, 528, 640), jnp.bfloat16),
            pltpu.VMEM((640, 9 * F), jnp.bfloat16),
            pltpu.VMEM((520, 9 * F), jnp.float32),
            pltpu.VMEM((F, 3 * C, F), jnp.bfloat16),
            pltpu.VMEM((F, 3 * C, F), jnp.bfloat16),
            pltpu.VMEM((F, 3 * C, F), jnp.bfloat16),
            pltpu.VMEM((5, C, F), jnp.float32),
            pltpu.SMEM((SLOTS,), jnp.int32),
            pltpu.SemaphoreType.DMA((2,)),
        ],
        out_shape=[
            jax.ShapeDtypeStruct((SLOTS, F, F), jnp.bfloat16),
            jax.ShapeDtypeStruct((SLOTS,), jnp.float32),
        ],
        compiler_params=pltpu.CompilerParams(vmem_limit_bytes=58 << 20),
    )(
        infos, framed, stem_weight, conv1_weight.reshape(9, C, C),
        conv2_weight.reshape(9, C, C), biases, head_weight.T, head_bias.reshape(1, 9),
    )
    return maps, logits


def blend_kernel(infos, maps, out_ref, total):
    out_ref[...] = jnp.zeros_like(out_ref)
    total[...] = jnp.zeros_like(total)

    def profile(offset):
        value = (offset - (WIN - 1) / 2.0) * (1.0 / (WIN / 4.0))
        return jnp.exp(-0.5 * value * value)

    def window(number, _):
        way, slot = number // SLOTS, number % SLOTS
        corner = infos[way, slot, 0]
        top = corner % TILE - way // 2 * TILE
        left = infos[way, slot, 1] % TILE - way % 2 * TILE

        @pl.when((corner >= 0) & (top > -WIN) & (left > -WIN))
        def _():
            row0 = pl.multiple_of(jnp.clip(top // 8 * 8, 0, TILE - 520), 8)
            col0 = pl.multiple_of(jnp.clip(left // F * F, 0, TILE - 640), F)
            row = lax.broadcasted_iota(jnp.int32, (520, F), 0) + (row0 - top)
            in_row = (row >= 0) & (row < WIN)
            up = jnp.where(in_row & (row // 4 == lanes((520, F))), 1.0, 0.0)
            down = jnp.where(in_row, profile(row.astype(jnp.float32)), 0.0)
            col = lanes((F, 640)) + (col0 - left)
            in_col = (col >= 0) & (col < WIN)
            tap = lax.broadcasted_iota(jnp.int32, (F, 640), 0)
            across = jnp.where(in_col & (col // 4 == tap), 1.0, 0.0).astype(jnp.bfloat16)
            col = lanes((8, 640)) + (col0 - left)
            in_col = (col >= 0) & (col < WIN)
            side = jnp.where(in_col, profile(col.astype(jnp.float32)), 0.0)[0:1]
            tall = jnp.dot(
                up.astype(jnp.bfloat16), maps[way, slot], preferred_element_type=jnp.float32
            ).astype(jnp.bfloat16)
            for k in range(5):
                part = slice(k * F, (k + 1) * F)
                at = (pl.ds(row0, 520), pl.ds(pl.multiple_of(col0 + k * F, F), F))
                weight = down * side[:, part]
                value = jnp.dot(tall, across[:, part], preferred_element_type=jnp.float32)
                out_ref[at] += value * weight
                total[at] += weight
        return 0

    lax.fori_loop(0, 4 * SLOTS, window, 0)
    out_ref[...] = out_ref[...] / jnp.maximum(total[...], 1.0)


def blend(infos, maps):
    return pl.pallas_call(
        blend_kernel,
        in_specs=[
            pl.BlockSpec(memory_space=pltpu.SMEM),
            pl.BlockSpec(memory_space=pltpu.VMEM),
        ],
        out_specs=pl.BlockSpec(memory_space=pltpu.VMEM),
        scratch_shapes=[pltpu.VMEM((TILE, TILE), jnp.float32)],
        out_shape=jax.ShapeDtypeStruct((TILE, TILE), jnp.float32),
        compiler_params=pltpu.CompilerParams(vmem_limit_bytes=40 << 20),
    )(infos, maps)


def share_kernel(maps, every, keep, send, recv):
    row, col = lax.axis_index("row"), lax.axis_index("col")
    rows, cols = lax.axis_size("row"), lax.axis_size("col")
    up, down, left, right = row > 0, row < rows - 1, col > 0, col < cols - 1
    own = pltpu.make_async_copy(maps, every.at[0], keep)
    own.start()
    goes = (right, down, down & right)
    comes = (left, up, up & left)
    barrier = pltpu.get_barrier_semaphore()
    for (by_row, by_col), out, back in zip(WAYS[1:], goes, comes):
        for sign, there in ((1, out), (-1, back)):
            @pl.when(there)
            def _():
                pl.semaphore_signal(
                    barrier, inc=1, device_id=(row + sign * by_row, col + sign * by_col),
                    device_id_type=MESH,
                )
    pl.semaphore_wait(barrier, sum(there.astype(jnp.int32) for there in goes + comes))
    copies = [
        pltpu.make_async_remote_copy(
            src_ref=maps, dst_ref=every.at[k], send_sem=send.at[k - 1], recv_sem=recv.at[k - 1],
            device_id=(row + WAYS[k][0], col + WAYS[k][1]), device_id_type=MESH,
        )
        for k in (1, 2, 3)
    ]
    for k in (2, 1, 0):
        pl.when(goes[k])(copies[k].start)
    own.wait()
    for k in range(3):
        pl.when(goes[k])(copies[k].wait_send)
        pl.when(comes[k])(copies[k].wait_recv)


def share(maps):
    return pl.pallas_call(
        share_kernel,
        out_shape=jax.ShapeDtypeStruct((4,) + maps.shape, maps.dtype),
        in_specs=[pl.BlockSpec(memory_space=pltpu.VMEM)],
        out_specs=pl.BlockSpec(memory_space=pltpu.VMEM),
        scratch_shapes=[
            pltpu.SemaphoreType.DMA,
            pltpu.SemaphoreType.DMA((3,)),
            pltpu.SemaphoreType.DMA((3,)),
        ],
        compiler_params=pltpu.CompilerParams(
            collective_id=1, has_side_effects=True, vmem_limit_bytes=40 << 20
        ),
    )(maps)


def local(scan, anchors, targets, *network):
    own = jnp.concatenate([anchors.reshape(SLOTS, 2), targets.reshape(SLOTS, 1)], 1)
    own = jnp.pad(own, ((0, 8 - SLOTS), (0, F - 3)), constant_values=-1)
    framed, infos = frame(scan, own)
    maps, scores = networks(infos, framed, *network)
    saliency = blend(infos, share(maps))
    return saliency, scores.reshape(targets.shape)


def solution(mesh):
    placed = (
        P("row", "col"),
        P(None, "row", "col", None),
        P(None, "row", "col"),
    ) + (P(),) * 8
    return jax.shard_map(
        local,
        mesh=mesh,
        in_specs=placed,
        out_specs=(P("row", "col"), P(None, "row", "col")),
        check_vma=False,
    )
```

```python
import jax
import jax.numpy as jnp
from jax import lax
from jax.experimental import pallas as pl
from jax.experimental.pallas import tpu as pltpu
from jax.sharding import PartitionSpec as P

TILE = 1024
WIN = 512
RIM = 512
C = 64
F = 128
SLOTS = 4
LOW = -3.0e38
MESH = pl.DeviceIdType.MESH
WAYS = ((0, 0), (0, 1), (1, 0), (1, 1))


def lanes(shape):
    return lax.broadcasted_iota(jnp.int32, shape, len(shape) - 1)


def frame_kernel(
    scan, own, framed, infos,
    raw, pixels, blank_rows, blank_cols, blanks, loads, keeps, up_send, up_recv, left_send, left_recv,
    corner_send, corner_recv, info_send, info_recv,
):
    row, col = lax.axis_index("row"), lax.axis_index("col")
    rows, cols = lax.axis_size("row"), lax.axis_size("col")
    up, down, left, right = row > 0, row < rows - 1, col > 0, col < cols - 1
    chunks = TILE // F
    fetch = [
        pltpu.make_async_copy(scan.at[pl.ds(k * F, F)], raw.at[pl.ds(k * F, F)], loads.at[k])
        for k in range(chunks)
    ]
    for copy in fetch:
        copy.start()
    infos[...] = jnp.full_like(infos, -1)
    infos[0] = own[...]

    blank_rows[...] = jnp.zeros_like(blank_rows)
    blank_cols[...] = jnp.zeros_like(blank_cols)

    def blank(source, k, by_rows, by_cols, there):
        return pltpu.make_async_copy(source, framed.at[by_rows, by_cols], blanks.at[k]), there

    edge, beyond = pl.ds(TILE, 16), pl.ds(TILE, F)
    no_down, no_right = row == rows - 1, col == cols - 1
    clears = (
        blank(blank_rows, 0, edge, pl.ds(0, TILE), no_down),
        blank(blank_rows.at[:, pl.ds(0, RIM)], 1, edge, pl.ds(TILE, RIM), no_down & right),
        blank(blank_cols, 2, pl.ds(0, TILE), beyond, no_right),
        blank(blank_cols.at[pl.ds(0, RIM)], 3, pl.ds(TILE, RIM), beyond, no_right),
    )
    for clear, there in clears:
        pl.when(there)(clear.start)

    barrier = pltpu.get_barrier_semaphore()
    partners = (
        (-1, 0, up), (1, 0, down), (0, -1, left), (0, 1, right),
        (1, 1, down & right), (-1, -1, up & left),
    )
    for by_row, by_col, there in partners:
        @pl.when(there)
        def _():
            pl.semaphore_signal(
                barrier, inc=1, device_id=(row + by_row, col + by_col), device_id_type=MESH
            )
    pl.semaphore_wait(barrier, sum(there.astype(jnp.int32) for _, _, there in partners))

    def remote(source, target, send, recv, by_row, by_col):
        return pltpu.make_async_remote_copy(
            src_ref=source, dst_ref=target, send_sem=send, recv_sem=recv,
            device_id=(row + by_row, col + by_col), device_id_type=MESH,
        )

    def part(k):
        return pl.ds(k * F, F)

    def under(k):
        return pl.ds(TILE + k * F, F)

    ups = [
        remote(pixels.at[part(k % 4), pl.ds(k // 4 * RIM, RIM)],
               framed.at[under(k % 4), pl.ds(k // 4 * RIM, RIM)],
               up_send.at[k], up_recv.at[k], -1, 0)
        for k in range(8)
    ]
    lefts = [
        remote(pixels.at[part(k), pl.ds(0, RIM)], framed.at[part(k), pl.ds(TILE, RIM)],
               left_send.at[k], left_recv.at[k], 0, -1)
        for k in range(chunks)
    ]
    corners = [
        remote(framed.at[under(k), pl.ds(0, RIM)], framed.at[under(k), pl.ds(TILE, RIM)],
               corner_send.at[k], corner_recv.at[k], 0, -1)
        for k in range(RIM // F)
    ]
    tells = [
        (remote(own, infos.at[1], info_send.at[0], info_recv.at[0], 0, 1), right, left),
        (remote(own, infos.at[2], info_send.at[1], info_recv.at[1], 1, 0), down, up),
        (remote(own, infos.at[3], info_send.at[2], info_recv.at[2], 1, 1), down & right, up & left),
    ]
    kept = [
        pltpu.make_async_copy(pixels.at[part(k)], framed.at[part(k), pl.ds(0, TILE)], keeps.at[k])
        for k in range(chunks)
    ]
    for k in range(chunks):
        fetch[k].wait()
        pixels[k * F : (k + 1) * F, :] = raw[k * F : (k + 1) * F, :].astype(jnp.bfloat16)
        if k < 4:
            pl.when(up)(ups[k].start)
        if k == 3:
            for late in ups[4:]:
                pl.when(up)(late.start)
        pl.when(left)(lefts[k].start)
        kept[k].start()
    for tell, goes, _ in tells:
        pl.when(goes)(tell.start)
    for k in range(len(ups)):
        pl.when(down)(ups[k].wait_recv)
        if k < len(corners):
            pl.when(down & left)(corners[k].start)
    for tell, goes, comes in tells:
        pl.when(goes)(tell.wait_send)
        pl.when(comes)(tell.wait_recv)
    for k in range(chunks):
        kept[k].wait()
        pl.when(left)(lefts[k].wait_send)
        pl.when(right)(lefts[k].wait_recv)
        pl.when(up)(ups[k].wait_send)
        if k < len(corners):
            pl.when(down & left)(corners[k].wait_send)
            pl.when(down & right)(corners[k].wait_recv)
    for clear, there in clears:
        pl.when(there)(clear.wait)


def frame(scan, own):
    chunks, rim = TILE // F, RIM // F
    sems = [4, chunks, chunks, 8, 8, chunks, chunks, rim, rim, 3, 3]
    return pl.pallas_call(
        frame_kernel,
        out_shape=[
            jax.ShapeDtypeStruct((TILE + RIM, TILE + RIM), jnp.bfloat16),
            jax.ShapeDtypeStruct((4, 8, F), jnp.int32),
        ],
        in_specs=[pl.BlockSpec(memory_space=pltpu.HBM), pl.BlockSpec(memory_space=pltpu.VMEM)],
        out_specs=[pl.BlockSpec(memory_space=pltpu.HBM), pl.BlockSpec(memory_space=pltpu.VMEM)],
        scratch_shapes=[
            pltpu.VMEM((TILE, TILE), jnp.float32),
            pltpu.VMEM((TILE, TILE), jnp.bfloat16),
            pltpu.VMEM((16, TILE), jnp.bfloat16),
            pltpu.VMEM((TILE, F), jnp.bfloat16),
        ] + [pltpu.SemaphoreType.DMA((n,)) for n in sems],
        compiler_params=pltpu.CompilerParams(
            collective_id=0, has_side_effects=True, vmem_limit_bytes=60 << 20
        ),
    )(scan, own)


def put_taps(ref, row, value):
    value = value.astype(jnp.bfloat16)
    lane = lanes((C, F))
    none = jnp.zeros((), jnp.bfloat16)
    ref[row, 0:C, :] = jnp.where(lane == 0, none, pltpu.roll(value, 1, 1))
    ref[row, C : 2 * C, :] = value
    ref[row, 2 * C : 3 * C, :] = jnp.where(lane == F - 1, none, pltpu.roll(value, F - 1, 1))


def convolved(taps_ref, weight_ref, finish):
    data = jnp.concatenate([taps_ref[k] for k in range(F)], 1)
    out = jnp.dot(weight_ref[...], data, preferred_element_type=jnp.float32)

    def part(tap, k):
        return out[tap * C : (tap + 1) * C, k * F : (k + 1) * F]

    for k in range(F):
        sums = part(1, k)
        if k > 0:
            sums = sums + part(0, k - 1)
        if k < F - 1:
            sums = sums + part(2, k + 1)
        finish(k, sums)


def arrange(stem_raw, first_raw, second_raw, biases_raw, stem_w, first_w, second_w, back_w, biases):
    taps = [stem_raw[k // 7, k % 7].astype(jnp.float32) for k in range(49)]
    turned = jnp.concatenate(taps, 0).T.astype(jnp.bfloat16)
    tap = lax.broadcasted_iota(jnp.int32, (49, 216), 0)
    tap_row, tap_col = tap // 7, tap % 7
    place_col, place_row = lanes((49, 216)) // 24, lanes((49, 216)) % 24
    for r in range(8):
        for q in range(2):
            hit = (place_row == 2 * r + tap_row) & (place_col == 2 * q + tap_col)
            hit = jnp.where(hit, 1.0, 0.0).astype(jnp.bfloat16)
            at = (r * 2 + q) * C
            stem_w[at : at + C, :] = jnp.dot(
                turned, hit, preferred_element_type=jnp.float32
            ).astype(jnp.bfloat16)
    for raw, laid in ((first_raw, first_w), (second_raw, second_w)):
        for dy in range(3):
            block = raw[dy * 3 : dy * 3 + 3].reshape(3 * C, C).astype(jnp.float32)
            laid[dy * C : (dy + 1) * C, :] = block.T.astype(jnp.bfloat16)
    for dy in range(3):
        blocks = [second_raw[(2 - dy) * 3 + (2 - dx)] for dx in range(3)]
        back_w[dy * C : (dy + 1) * C, :] = jnp.concatenate(blocks, 1)
    eye = lax.broadcasted_iota(jnp.int32, (C, C), 0) == lanes((C, C))
    for k in range(3):
        upright = jnp.sum(jnp.where(eye, biases_raw[k : k + 1, :], 0.0), 1, keepdims=True)
        biases[k] = jnp.broadcast_to(upright, (C, F))


def net_kernel(
    infos, source, stem_raw, first_raw, second_raw, biases_raw, heads, head_bias,
    map_ref, logit_ref,
    stem_w, first_w, second_w, back_w, biases,
    pixels, spread_ref, picked, feats, hidden, grads, acc, order, arrival,
):
    count = jnp.int32(0)
    for slot in range(SLOTS):
        live = infos[0, slot, 0] >= 0

        @pl.when(live)
        def _():
            order[count] = slot

        count = count + live.astype(jnp.int32)

    def place(number):
        slot = order[number]
        return slot, infos[0, slot, 0] % TILE, infos[0, slot, 1] % TILE, infos[0, slot, 2]

    def fetch(number):
        _, top, left, _ = place(number)
        row0 = pl.multiple_of(top // 16 * 16, 16)
        col0 = pl.multiple_of(left // F * F, F)
        here = number % 2
        return pltpu.make_async_copy(
            source.at[pl.ds(row0, 528), pl.ds(col0, 640)], pixels.at[here], arrival.at[here]
        )

    @pl.when(count > 0)
    def _():
        fetch(0).start()

    arrange(
        stem_raw, first_raw, second_raw, biases_raw, stem_w, first_w, second_w, back_w, biases
    )
    map_ref[...] = jnp.zeros_like(map_ref)
    for slot in range(SLOTS):
        logit_ref[slot] = jnp.float32(0.0)

    def window(number, _):
        slot, top, left, target = place(number)

        @pl.when(number + 1 < count)
        def _():
            fetch(number + 1).start()

        over = left % F
        lane = lanes((640, F))
        apart = lax.broadcasted_iota(jnp.int32, (640, F), 0) - over - lane * 4
        for u in range(9):
            hit = apart == u - 3
            if u < 3:
                hit = hit & (lane > 0)
            if u > 6:
                hit = hit & (lane < F - 1)
            spread_ref[:, u * F : (u + 1) * F] = jnp.where(hit, 1.0, 0.0).astype(jnp.bfloat16)
        below = top % 16
        row = lax.broadcasted_iota(jnp.int32, (520, 528), 0) - 3
        shift = jnp.where(
            (lanes((520, 528)) - below == row) & (row >= 0) & (row < WIN), 1.0, 0.0
        ).astype(jnp.bfloat16)
        fetch(number).wait()
        moved = jnp.dot(shift, pixels[number % 2], preferred_element_type=jnp.float32)
        picked[...] = jnp.dot(
            moved.astype(jnp.bfloat16), spread_ref[...], preferred_element_type=jnp.float32
        )
        stem_bias = biases[0]
        lane0 = lanes((C, F)) == 0
        none = jnp.zeros((), jnp.bfloat16)

        def stem():
            even = odd = jnp.full((C, F), LOW, jnp.float32)
            slabs = []
            for k in range(F // 4):
                slab = [
                    picked[k * 16 : k * 16 + 24, u * F : (u + 1) * F] for u in range(9)
                ]
                slabs.append(jnp.concatenate(slab, 0))
            data = jnp.concatenate(slabs, 1).astype(jnp.bfloat16)
            out = jnp.dot(stem_w[...], data, preferred_element_type=jnp.float32)
            for k in range(F // 4):
                for r in range(4):
                    part = lambda n: out[
                        (r * 4 + n) * C : (r * 4 + n + 1) * C, k * F : (k + 1) * F
                    ]
                    e_high = jnp.maximum(jnp.maximum(even, part(0)), part(2))
                    o_high = jnp.maximum(jnp.maximum(odd, part(1)), part(3))
                    even, odd = part(2), part(3)
                    high = jnp.maximum(e_high, o_high) + stem_bias
                    high = jnp.maximum(high, 0.0).astype(jnp.bfloat16)
                    side = jnp.maximum(o_high + stem_bias, 0.0).astype(jnp.bfloat16)
                    before = jnp.where(lane0, none, pltpu.roll(side, 1, 1))
                    put_taps(feats, k * 4 + r, jnp.maximum(high, before))

        stem()

        def after_first(row, sums):
            put_taps(hidden, row, jnp.maximum(sums + biases[1], 0.0))

        convolved(feats, first_w, after_first)

        eye = lax.broadcasted_iota(jnp.int32, (C, C), 0) == lanes((C, C))
        wanted = lax.broadcasted_iota(jnp.int32, (9, C), 0) == target
        head = jnp.where(wanted, heads[...].astype(jnp.float32), 0.0)
        head = jnp.sum(head, 0, keepdims=True)
        column = jnp.sum(jnp.where(eye, head, 0.0), 1, keepdims=True)
        grad = jnp.broadcast_to(
            (column / float(F * F)).astype(jnp.bfloat16).astype(jnp.float32), (C, F)
        )
        acc[...] = jnp.zeros_like(acc)
        held = []

        def after_second(row, sums):
            value = sums + feats[row, C : 2 * C, :].astype(jnp.float32) + biases[2]
            value = jnp.maximum(value, 0.0)
            out = jnp.where(value > 0, grad, 0.0)
            put_taps(grads, row, out)
            held.append((value, out))
            if len(held) == 4:
                acc[0] += (held[0][0] + held[1][0]) + (held[2][0] + held[3][0])
                acc[1] += (held[0][1] + held[1][1]) + (held[2][1] + held[3][1])
                held.clear()

        convolved(hidden, second_w, after_second)

        def after_back(row, sums):
            open_ = hidden[row, C : 2 * C, :].astype(jnp.float32) > 0
            value = jnp.where(open_, sums, 0.0).astype(jnp.bfloat16).astype(jnp.float32)
            if row == 0:
                acc[3] = value
            if row == F - 1:
                acc[4] = value
            held.append(value)
            if len(held) == 4:
                acc[2] += (held[0] + held[1]) + (held[2] + held[3])
                held.clear()

        convolved(grads, back_w, after_back)

        mean = jnp.sum(acc[0], 1, keepdims=True) / float(F * F)
        logit = jnp.sum(mean * column)
        bias = jnp.sum(jnp.where(lanes((1, 9)) == target, head_bias[...], 0.0))
        logit_ref[slot] = logit + bias

        whole = acc[2]
        parts = [whole - acc[4], whole, whole - acc[3]]
        lane = lanes((C, F))
        channel = jnp.sum(acc[1], 1, keepdims=True)
        for dy in range(3):
            for dx in range(3):
                drop = {0: F - 1, 1: F, 2: 0}[dx]
                total = jnp.sum(jnp.where(lane == drop, 0.0, parts[dy]), 1, keepdims=True)
                flat = jnp.sum(jnp.where(eye, total, 0.0), 0, keepdims=True)
                weight = first_raw[(2 - dy) * 3 + (2 - dx)].astype(jnp.float32)
                channel = channel + jnp.sum(weight * flat, 1, keepdims=True)
        channel = jnp.broadcast_to(channel, (C, F))

        def rows(step, _):
            base = pl.multiple_of(step * 16, 16)
            found = [
                jnp.sum(
                    feats[base + k, C : 2 * C, :].astype(jnp.float32) * channel, 0, keepdims=True
                )
                for k in range(16)
            ]
            found = jnp.maximum(jnp.concatenate(found, 0), 0.0)
            map_ref[slot, pl.ds(base, 16), :] = found.astype(jnp.bfloat16)
            return 0

        lax.fori_loop(0, F // 16, rows, 0)
        return 0

    lax.fori_loop(0, count, window, 0)


def networks(infos, framed, stem_weight, stem_bias, conv1_weight, conv1_bias, conv2_weight,
             conv2_bias, head_weight, head_bias):
    biases = jnp.stack([stem_bias, conv1_bias, conv2_bias])
    whole = pl.BlockSpec(memory_space=pltpu.VMEM)
    maps, logits = pl.pallas_call(
        net_kernel,
        in_specs=[pl.BlockSpec(memory_space=pltpu.SMEM), pl.BlockSpec(memory_space=pltpu.HBM)]
        + [whole] * 6,
        out_specs=[whole, pl.BlockSpec(memory_space=pltpu.SMEM)],
        scratch_shapes=[
            pltpu.VMEM((16 * C, 216), jnp.bfloat16),
            pltpu.VMEM((3 * C, 3 * C), jnp.bfloat16),
            pltpu.VMEM((3 * C, 3 * C), jnp.bfloat16),
            pltpu.VMEM((3 * C, 3 * C), jnp.bfloat16),
            pltpu.VMEM((3, C, F), jnp.float32),
            pltpu.VMEM((2, 528, 640), jnp.bfloat16),
            pltpu.VMEM((640, 9 * F), jnp.bfloat16),
            pltpu.VMEM((520, 9 * F), jnp.float32),
            pltpu.VMEM((F, 3 * C, F), jnp.bfloat16),
            pltpu.VMEM((F, 3 * C, F), jnp.bfloat16),
            pltpu.VMEM((F, 3 * C, F), jnp.bfloat16),
            pltpu.VMEM((5, C, F), jnp.float32),
            pltpu.SMEM((SLOTS,), jnp.int32),
            pltpu.SemaphoreType.DMA((2,)),
        ],
        out_shape=[
            jax.ShapeDtypeStruct((SLOTS, F, F), jnp.bfloat16),
            jax.ShapeDtypeStruct((SLOTS,), jnp.float32),
        ],
        compiler_params=pltpu.CompilerParams(vmem_limit_bytes=58 << 20),
    )(
        infos, framed, stem_weight, conv1_weight.reshape(9, C, C),
        conv2_weight.reshape(9, C, C), biases, head_weight.T, head_bias.reshape(1, 9),
    )
    return maps, logits


def blend_kernel(infos, maps, result, out_ref, total, sems):
    out_ref[...] = jnp.zeros_like(out_ref)
    total[...] = jnp.zeros_like(total)

    def profile(offset):
        value = (offset - (WIN - 1) / 2.0) * (1.0 / (WIN / 4.0))
        return jnp.exp(-0.5 * value * value)

    def window(number, _):
        way, slot = number // SLOTS, number % SLOTS
        corner = infos[way, slot, 0]
        top = corner % TILE - way // 2 * TILE
        left = infos[way, slot, 1] % TILE - way % 2 * TILE

        @pl.when((corner >= 0) & (top > -WIN) & (left > -WIN))
        def _():
            row0 = pl.multiple_of(jnp.clip(top // 8 * 8, 0, TILE - 520), 8)
            col0 = pl.multiple_of(jnp.clip(left // F * F, 0, TILE - 640), F)
            row = lax.broadcasted_iota(jnp.int32, (520, F), 0) + (row0 - top)
            in_row = (row >= 0) & (row < WIN)
            up = jnp.where(in_row & (row // 4 == lanes((520, F))), 1.0, 0.0)
            down = jnp.where(in_row, profile(row.astype(jnp.float32)), 0.0)
            col = lanes((F, 640)) + (col0 - left)
            in_col = (col >= 0) & (col < WIN)
            tap = lax.broadcasted_iota(jnp.int32, (F, 640), 0)
            across = jnp.where(in_col & (col // 4 == tap), 1.0, 0.0).astype(jnp.bfloat16)
            col = lanes((8, 640)) + (col0 - left)
            in_col = (col >= 0) & (col < WIN)
            side = jnp.where(in_col, profile(col.astype(jnp.float32)), 0.0)[0:1]
            tall = jnp.dot(
                up.astype(jnp.bfloat16), maps[way, slot], preferred_element_type=jnp.float32
            ).astype(jnp.bfloat16)
            for k in range(5):
                part = slice(k * F, (k + 1) * F)
                at = (pl.ds(row0, 520), pl.ds(pl.multiple_of(col0 + k * F, F), F))
                weight = down * side[:, part]
                value = jnp.dot(tall, across[:, part], preferred_element_type=jnp.float32)
                out_ref[at] += value * weight
                total[at] += weight
        return 0

    lax.fori_loop(0, 4 * SLOTS, window, 0)
    copies = []
    for k in range(TILE // F):
        part = slice(k * F, (k + 1) * F)
        out_ref[part, :] = out_ref[part, :] / jnp.maximum(total[part, :], 1.0)
        rows = pl.ds(k * F, F)
        copies.append(pltpu.make_async_copy(out_ref.at[rows], result.at[rows], sems.at[k]))
        copies[-1].start()
    for copy in copies:
        copy.wait()


def blend(infos, maps):
    return pl.pallas_call(
        blend_kernel,
        in_specs=[
            pl.BlockSpec(memory_space=pltpu.SMEM),
            pl.BlockSpec(memory_space=pltpu.VMEM),
        ],
        out_specs=pl.BlockSpec(memory_space=pltpu.HBM),
        scratch_shapes=[
            pltpu.VMEM((TILE, TILE), jnp.float32),
            pltpu.VMEM((TILE, TILE), jnp.float32),
            pltpu.SemaphoreType.DMA((TILE // F,)),
        ],
        out_shape=jax.ShapeDtypeStruct((TILE, TILE), jnp.float32),
        compiler_params=pltpu.CompilerParams(vmem_limit_bytes=40 << 20),
    )(infos, maps)


def share_kernel(maps, every, keep, send, recv):
    row, col = lax.axis_index("row"), lax.axis_index("col")
    rows, cols = lax.axis_size("row"), lax.axis_size("col")
    up, down, left, right = row > 0, row < rows - 1, col > 0, col < cols - 1
    own = pltpu.make_async_copy(maps, every.at[0], keep)
    own.start()
    goes = (right, down, down & right)
    comes = (left, up, up & left)
    barrier = pltpu.get_barrier_semaphore()
    for (by_row, by_col), out, back in zip(WAYS[1:], goes, comes):
        for sign, there in ((1, out), (-1, back)):
            @pl.when(there)
            def _():
                pl.semaphore_signal(
                    barrier, inc=1, device_id=(row + sign * by_row, col + sign * by_col),
                    device_id_type=MESH,
                )
    pl.semaphore_wait(barrier, sum(there.astype(jnp.int32) for there in goes + comes))
    copies = [
        pltpu.make_async_remote_copy(
            src_ref=maps, dst_ref=every.at[k], send_sem=send.at[k - 1], recv_sem=recv.at[k - 1],
            device_id=(row + WAYS[k][0], col + WAYS[k][1]), device_id_type=MESH,
        )
        for k in (1, 2, 3)
    ]
    for k in (2, 1, 0):
        pl.when(goes[k])(copies[k].start)
    own.wait()
    for k in range(3):
        pl.when(goes[k])(copies[k].wait_send)
        pl.when(comes[k])(copies[k].wait_recv)


def share(maps):
    return pl.pallas_call(
        share_kernel,
        out_shape=jax.ShapeDtypeStruct((4,) + maps.shape, maps.dtype),
        in_specs=[pl.BlockSpec(memory_space=pltpu.VMEM)],
        out_specs=pl.BlockSpec(memory_space=pltpu.VMEM),
        scratch_shapes=[
            pltpu.SemaphoreType.DMA,
            pltpu.SemaphoreType.DMA((3,)),
            pltpu.SemaphoreType.DMA((3,)),
        ],
        compiler_params=pltpu.CompilerParams(
            collective_id=1, has_side_effects=True, vmem_limit_bytes=40 << 20
        ),
    )(maps)


def local(scan, anchors, targets, *network):
    own = jnp.concatenate([anchors.reshape(SLOTS, 2), targets.reshape(SLOTS, 1)], 1)
    own = jnp.pad(own, ((0, 8 - SLOTS), (0, F - 3)), constant_values=-1)
    framed, infos = frame(scan, own)
    maps, scores = networks(infos, framed, *network)
    saliency = blend(infos, share(maps))
    return saliency, scores.reshape(targets.shape)


def solution(mesh):
    placed = (
        P("row", "col"),
        P(None, "row", "col", None),
        P(None, "row", "col"),
    ) + (P(),) * 8
    return jax.shard_map(
        local,
        mesh=mesh,
        in_specs=placed,
        out_specs=(P("row", "col"), P(None, "row", "col")),
        check_vma=False,
    )
```

```python
import jax
import jax.numpy as jnp
from jax import lax
from jax.experimental import pallas as pl
from jax.experimental.pallas import tpu as pltpu
from jax.sharding import PartitionSpec as P

TILE = 1024
WIN = 512
RIM = 512
C = 64
F = 128
SLOTS = 4
LOW = -3.0e38
MESH = pl.DeviceIdType.MESH
WAYS = ((0, 0), (0, 1), (1, 0), (1, 1))


def lanes(shape):
    return lax.broadcasted_iota(jnp.int32, shape, len(shape) - 1)


def frame_kernel(
    scan, own, framed, infos,
    raw, pixels, blank_rows, blank_cols, blanks, loads, keeps, up_send, up_recv, left_send, left_recv,
    corner_send, corner_recv, info_send, info_recv,
):
    row, col = lax.axis_index("row"), lax.axis_index("col")
    rows, cols = lax.axis_size("row"), lax.axis_size("col")
    up, down, left, right = row > 0, row < rows - 1, col > 0, col < cols - 1
    chunks = TILE // F
    fetch = [
        pltpu.make_async_copy(scan.at[pl.ds(k * F, F)], raw.at[pl.ds(k * F, F)], loads.at[k])
        for k in range(chunks)
    ]
    for copy in fetch:
        copy.start()
    infos[...] = jnp.full_like(infos, -1)
    infos[0] = own[...]

    blank_rows[...] = jnp.zeros_like(blank_rows)
    blank_cols[...] = jnp.zeros_like(blank_cols)

    def blank(source, k, by_rows, by_cols, there):
        return pltpu.make_async_copy(source, framed.at[by_rows, by_cols], blanks.at[k]), there

    edge, beyond = pl.ds(TILE, 16), pl.ds(TILE, F)
    no_down, no_right = row == rows - 1, col == cols - 1
    clears = (
        blank(blank_rows, 0, edge, pl.ds(0, TILE), no_down),
        blank(blank_rows.at[:, pl.ds(0, RIM)], 1, edge, pl.ds(TILE, RIM), no_down & right),
        blank(blank_cols, 2, pl.ds(0, TILE), beyond, no_right),
        blank(blank_cols.at[pl.ds(0, RIM)], 3, pl.ds(TILE, RIM), beyond, no_right),
    )
    for clear, there in clears:
        pl.when(there)(clear.start)

    barrier = pltpu.get_barrier_semaphore()
    partners = (
        (-1, 0, up), (1, 0, down), (0, -1, left), (0, 1, right),
        (1, 1, down & right), (-1, -1, up & left),
    )
    for by_row, by_col, there in partners:
        @pl.when(there)
        def _():
            pl.semaphore_signal(
                barrier, inc=1, device_id=(row + by_row, col + by_col), device_id_type=MESH
            )
    pl.semaphore_wait(barrier, sum(there.astype(jnp.int32) for _, _, there in partners))

    def remote(source, target, send, recv, by_row, by_col):
        return pltpu.make_async_remote_copy(
            src_ref=source, dst_ref=target, send_sem=send, recv_sem=recv,
            device_id=(row + by_row, col + by_col), device_id_type=MESH,
        )

    def part(k):
        return pl.ds(k * F, F)

    def under(k):
        return pl.ds(TILE + k * F, F)

    ups = [
        remote(pixels.at[part(k % 4), pl.ds(k // 4 * RIM, RIM)],
               framed.at[under(k % 4), pl.ds(k // 4 * RIM, RIM)],
               up_send.at[k], up_recv.at[k], -1, 0)
        for k in range(8)
    ]
    lefts = [
        remote(pixels.at[part(k), pl.ds(0, RIM)], framed.at[part(k), pl.ds(TILE, RIM)],
               left_send.at[k], left_recv.at[k], 0, -1)
        for k in range(chunks)
    ]
    corners = [
        remote(framed.at[under(k), pl.ds(0, RIM)], framed.at[under(k), pl.ds(TILE, RIM)],
               corner_send.at[k], corner_recv.at[k], 0, -1)
        for k in range(RIM // F)
    ]
    tells = [
        (remote(own, infos.at[1], info_send.at[0], info_recv.at[0], 0, 1), right, left),
        (remote(own, infos.at[2], info_send.at[1], info_recv.at[1], 1, 0), down, up),
        (remote(own, infos.at[3], info_send.at[2], info_recv.at[2], 1, 1), down & right, up & left),
    ]
    kept = [
        pltpu.make_async_copy(pixels.at[part(k)], framed.at[part(k), pl.ds(0, TILE)], keeps.at[k])
        for k in range(chunks)
    ]
    for k in range(chunks):
        fetch[k].wait()
        pixels[k * F : (k + 1) * F, :] = raw[k * F : (k + 1) * F, :].astype(jnp.bfloat16)
        if k < 4:
            pl.when(up)(ups[k].start)
        if k == 3:
            for late in ups[4:]:
                pl.when(up)(late.start)
        pl.when(left)(lefts[k].start)
        kept[k].start()
    for tell, goes, _ in tells:
        pl.when(goes)(tell.start)
    for k in range(len(ups)):
        pl.when(down)(ups[k].wait_recv)
        if k < len(corners):
            pl.when(down & left)(corners[k].start)
    for tell, goes, comes in tells:
        pl.when(goes)(tell.wait_send)
        pl.when(comes)(tell.wait_recv)
    for k in range(chunks):
        kept[k].wait()
        pl.when(left)(lefts[k].wait_send)
        pl.when(right)(lefts[k].wait_recv)
        pl.when(up)(ups[k].wait_send)
        if k < len(corners):
            pl.when(down & left)(corners[k].wait_send)
            pl.when(down & right)(corners[k].wait_recv)
    for clear, there in clears:
        pl.when(there)(clear.wait)


def frame(scan, own):
    chunks, rim = TILE // F, RIM // F
    sems = [4, chunks, chunks, 8, 8, chunks, chunks, rim, rim, 3, 3]
    return pl.pallas_call(
        frame_kernel,
        out_shape=[
            jax.ShapeDtypeStruct((TILE + RIM, TILE + RIM), jnp.bfloat16),
            jax.ShapeDtypeStruct((4,) + own.shape, jnp.int32),
        ],
        in_specs=[pl.BlockSpec(memory_space=pltpu.HBM), pl.BlockSpec(memory_space=pltpu.VMEM)],
        out_specs=[pl.BlockSpec(memory_space=pltpu.HBM), pl.BlockSpec(memory_space=pltpu.VMEM)],
        scratch_shapes=[
            pltpu.VMEM((TILE, TILE), jnp.float32),
            pltpu.VMEM((TILE, TILE), jnp.bfloat16),
            pltpu.VMEM((16, TILE), jnp.bfloat16),
            pltpu.VMEM((TILE, F), jnp.bfloat16),
        ] + [pltpu.SemaphoreType.DMA((n,)) for n in sems],
        compiler_params=pltpu.CompilerParams(
            collective_id=0, has_side_effects=True, vmem_limit_bytes=60 << 20
        ),
    )(scan, own)


def put_taps(ref, row, value):
    value = value.astype(jnp.bfloat16)
    lane = lanes((C, F))
    none = jnp.zeros((), jnp.bfloat16)
    ref[row, 0:C, :] = jnp.where(lane == 0, none, pltpu.roll(value, 1, 1))
    ref[row, C : 2 * C, :] = value
    ref[row, 2 * C : 3 * C, :] = jnp.where(lane == F - 1, none, pltpu.roll(value, F - 1, 1))


def convolved(taps_ref, weight_ref, finish):
    data = jnp.concatenate([taps_ref[k] for k in range(F)], 1)
    out = jnp.dot(weight_ref[...], data, preferred_element_type=jnp.float32)

    def part(tap, k):
        return out[tap * C : (tap + 1) * C, k * F : (k + 1) * F]

    for k in range(F):
        sums = part(1, k)
        if k > 0:
            sums = sums + part(0, k - 1)
        if k < F - 1:
            sums = sums + part(2, k + 1)
        finish(k, sums)


def arrange(stem_raw, first_raw, second_raw, biases_raw, stem_w, first_w, second_w, back_w, biases):
    taps = [stem_raw[k // 7, k % 7].astype(jnp.float32) for k in range(49)]
    turned = jnp.concatenate(taps, 0).T.astype(jnp.bfloat16)
    tap = lax.broadcasted_iota(jnp.int32, (49, 216), 0)
    tap_row, tap_col = tap // 7, tap % 7
    place_col, place_row = lanes((49, 216)) // 24, lanes((49, 216)) % 24
    for r in range(8):
        for q in range(2):
            hit = (place_row == 2 * r + tap_row) & (place_col == 2 * q + tap_col)
            hit = jnp.where(hit, 1.0, 0.0).astype(jnp.bfloat16)
            at = (r * 2 + q) * C
            stem_w[at : at + C, :] = jnp.dot(
                turned, hit, preferred_element_type=jnp.float32
            ).astype(jnp.bfloat16)
    for raw, laid in ((first_raw, first_w), (second_raw, second_w)):
        for dy in range(3):
            block = raw[dy * 3 : dy * 3 + 3].reshape(3 * C, C).astype(jnp.float32)
            laid[dy * C : (dy + 1) * C, :] = block.T.astype(jnp.bfloat16)
    for dy in range(3):
        blocks = [second_raw[(2 - dy) * 3 + (2 - dx)] for dx in range(3)]
        back_w[dy * C : (dy + 1) * C, :] = jnp.concatenate(blocks, 1)
    eye = lax.broadcasted_iota(jnp.int32, (C, C), 0) == lanes((C, C))
    for k in range(3):
        upright = jnp.sum(jnp.where(eye, biases_raw[k][...], 0.0), 1, keepdims=True)
        biases[k] = jnp.broadcast_to(upright, (C, F))


def net_kernel(
    infos, targets, source, stem_raw, first_raw, second_raw,
    stem_bias_raw, first_bias_raw, second_bias_raw, heads, head_bias,
    map_ref, logit_ref,
    stem_w, first_w, second_w, back_w, biases,
    pixels, spread_ref, picked, feats, hidden, grads, acc, order, arrival,
):
    count = jnp.int32(0)
    for slot in range(SLOTS):
        live = infos[0, slot // 2, slot % 2, 0, 0] >= 0

        @pl.when(live)
        def _():
            order[count] = slot

        count = count + live.astype(jnp.int32)

    def place(number):
        slot = order[number]
        turn, which = slot // 2, slot % 2
        top, left = (infos[0, turn, which, 0, k] % TILE for k in range(2))
        return slot, top, left, targets[turn, which, 0]

    def fetch(number):
        _, top, left, _ = place(number)
        row0 = pl.multiple_of(top // 16 * 16, 16)
        col0 = pl.multiple_of(left // F * F, F)
        here = number % 2
        return pltpu.make_async_copy(
            source.at[pl.ds(row0, 528), pl.ds(col0, 640)], pixels.at[here], arrival.at[here]
        )

    @pl.when(count > 0)
    def _():
        fetch(0).start()

    biases_raw = (stem_bias_raw, first_bias_raw, second_bias_raw)
    arrange(
        stem_raw, first_raw, second_raw, biases_raw, stem_w, first_w, second_w, back_w, biases
    )
    map_ref[...] = jnp.zeros_like(map_ref)
    for slot in range(SLOTS):
        logit_ref[slot] = jnp.float32(0.0)

    def window(number, _):
        slot, top, left, target = place(number)

        @pl.when(number + 1 < count)
        def _():
            fetch(number + 1).start()

        over = left % F
        lane = lanes((640, F))
        apart = lax.broadcasted_iota(jnp.int32, (640, F), 0) - over - lane * 4
        for u in range(9):
            hit = apart == u - 3
            if u < 3:
                hit = hit & (lane > 0)
            if u > 6:
                hit = hit & (lane < F - 1)
            spread_ref[:, u * F : (u + 1) * F] = jnp.where(hit, 1.0, 0.0).astype(jnp.bfloat16)
        below = top % 16
        row = lax.broadcasted_iota(jnp.int32, (520, 528), 0) - 3
        shift = jnp.where(
            (lanes((520, 528)) - below == row) & (row >= 0) & (row < WIN), 1.0, 0.0
        ).astype(jnp.bfloat16)
        fetch(number).wait()
        moved = jnp.dot(shift, pixels[number % 2], preferred_element_type=jnp.float32)
        picked[...] = jnp.dot(
            moved.astype(jnp.bfloat16), spread_ref[...], preferred_element_type=jnp.float32
        )
        stem_bias = biases[0]
        lane0 = lanes((C, F)) == 0
        none = jnp.zeros((), jnp.bfloat16)

        def stem():
            even = odd = jnp.full((C, F), LOW, jnp.float32)
            slabs = []
            for k in range(F // 4):
                slab = [
                    picked[k * 16 : k * 16 + 24, u * F : (u + 1) * F] for u in range(9)
                ]
                slabs.append(jnp.concatenate(slab, 0))
            data = jnp.concatenate(slabs, 1).astype(jnp.bfloat16)
            out = jnp.dot(stem_w[...], data, preferred_element_type=jnp.float32)
            for k in range(F // 4):
                for r in range(4):
                    part = lambda n: out[
                        (r * 4 + n) * C : (r * 4 + n + 1) * C, k * F : (k + 1) * F
                    ]
                    e_high = jnp.maximum(jnp.maximum(even, part(0)), part(2))
                    o_high = jnp.maximum(jnp.maximum(odd, part(1)), part(3))
                    even, odd = part(2), part(3)
                    high = jnp.maximum(e_high, o_high) + stem_bias
                    high = jnp.maximum(high, 0.0).astype(jnp.bfloat16)
                    side = jnp.maximum(o_high + stem_bias, 0.0).astype(jnp.bfloat16)
                    before = jnp.where(lane0, none, pltpu.roll(side, 1, 1))
                    put_taps(feats, k * 4 + r, jnp.maximum(high, before))

        stem()

        def after_first(row, sums):
            put_taps(hidden, row, jnp.maximum(sums + biases[1], 0.0))

        convolved(feats, first_w, after_first)

        eye = lax.broadcasted_iota(jnp.int32, (C, C), 0) == lanes((C, C))
        wanted = lax.broadcasted_iota(jnp.int32, (9, C), 0) == target
        head = jnp.where(wanted, heads[...].astype(jnp.float32), 0.0)
        head = jnp.sum(head, 0, keepdims=True)
        column = jnp.sum(jnp.where(eye, head, 0.0), 1, keepdims=True)
        grad = jnp.broadcast_to(
            (column / float(F * F)).astype(jnp.bfloat16).astype(jnp.float32), (C, F)
        )
        acc[...] = jnp.zeros_like(acc)
        held = []

        def after_second(row, sums):
            value = sums + feats[row, C : 2 * C, :].astype(jnp.float32) + biases[2]
            value = jnp.maximum(value, 0.0)
            out = jnp.where(value > 0, grad, 0.0)
            put_taps(grads, row, out)
            held.append((value, out))
            if len(held) == 8:
                acc[0] += sum(kept for kept, _ in held)
                acc[1] += sum(kept for _, kept in held)
                held.clear()

        convolved(hidden, second_w, after_second)

        def after_back(row, sums):
            open_ = hidden[row, C : 2 * C, :].astype(jnp.float32) > 0
            value = jnp.where(open_, sums, 0.0).astype(jnp.bfloat16).astype(jnp.float32)
            if row == 0:
                acc[3] = value
            if row == F - 1:
                acc[4] = value
            held.append(value)
            if len(held) == 8:
                acc[2] += sum(held)
                held.clear()

        convolved(grads, back_w, after_back)

        mean = jnp.sum(acc[0], 1, keepdims=True) / float(F * F)
        logit = jnp.sum(mean * column)
        bias = jnp.sum(jnp.where(lanes((1, 9)) == target, head_bias[...], 0.0))
        logit_ref[slot] = logit + bias

        whole = acc[2]
        parts = [whole - acc[4], whole, whole - acc[3]]
        lane = lanes((C, F))
        channel = jnp.sum(acc[1], 1, keepdims=True)
        for dy in range(3):
            for dx in range(3):
                drop = {0: F - 1, 1: F, 2: 0}[dx]
                total = jnp.sum(jnp.where(lane == drop, 0.0, parts[dy]), 1, keepdims=True)
                flat = jnp.sum(jnp.where(eye, total, 0.0), 0, keepdims=True)
                weight = first_raw[(2 - dy) * 3 + (2 - dx)].astype(jnp.float32)
                channel = channel + jnp.sum(weight * flat, 1, keepdims=True)
        channel = jnp.broadcast_to(channel, (C, F))

        def rows(step, _):
            base = pl.multiple_of(step * 16, 16)
            found = [
                jnp.sum(
                    feats[base + k, C : 2 * C, :].astype(jnp.float32) * channel, 0, keepdims=True
                )
                for k in range(16)
            ]
            found = jnp.maximum(jnp.concatenate(found, 0), 0.0)
            map_ref[slot, pl.ds(base, 16), :] = found.astype(jnp.bfloat16)
            return 0

        lax.fori_loop(0, F // 16, rows, 0)
        return 0

    lax.fori_loop(0, count, window, 0)


def networks(infos, targets, framed, stem_weight, stem_bias, conv1_weight, conv1_bias, conv2_weight,
             conv2_bias, head_weight, head_bias):
    biases = [bias.reshape(1, C) for bias in (stem_bias, conv1_bias, conv2_bias)]
    whole = pl.BlockSpec(memory_space=pltpu.VMEM)
    maps, logits = pl.pallas_call(
        net_kernel,
        in_specs=[pl.BlockSpec(memory_space=pltpu.SMEM)] * 2
        + [pl.BlockSpec(memory_space=pltpu.HBM)] + [whole] * 8,
        out_specs=[whole, pl.BlockSpec(memory_space=pltpu.SMEM)],
        scratch_shapes=[
            pltpu.VMEM((16 * C, 216), jnp.bfloat16),
            pltpu.VMEM((3 * C, 3 * C), jnp.bfloat16),
            pltpu.VMEM((3 * C, 3 * C), jnp.bfloat16),
            pltpu.VMEM((3 * C, 3 * C), jnp.bfloat16),
            pltpu.VMEM((3, C, F), jnp.float32),
            pltpu.VMEM((2, 528, 640), jnp.bfloat16),
            pltpu.VMEM((640, 9 * F), jnp.bfloat16),
            pltpu.VMEM((520, 9 * F), jnp.float32),
            pltpu.VMEM((F, 3 * C, F), jnp.bfloat16),
            pltpu.VMEM((F, 3 * C, F), jnp.bfloat16),
            pltpu.VMEM((F, 3 * C, F), jnp.bfloat16),
            pltpu.VMEM((5, C, F), jnp.float32),
            pltpu.SMEM((SLOTS,), jnp.int32),
            pltpu.SemaphoreType.DMA((2,)),
        ],
        out_shape=[
            jax.ShapeDtypeStruct((SLOTS, F, F), jnp.bfloat16),
            jax.ShapeDtypeStruct((SLOTS,), jnp.float32),
        ],
        compiler_params=pltpu.CompilerParams(vmem_limit_bytes=58 << 20),
    )(
        infos, targets, framed, stem_weight, conv1_weight.reshape(9, C, C),
        conv2_weight.reshape(9, C, C), *biases, head_weight.T, head_bias.reshape(1, 9),
    )
    return maps, logits


def blend_kernel(infos, maps, result, out_ref, total, sems):
    out_ref[...] = jnp.zeros_like(out_ref)
    total[...] = jnp.zeros_like(total)

    def profile(offset):
        value = (offset - (WIN - 1) / 2.0) * (1.0 / (WIN / 4.0))
        return jnp.exp(-0.5 * value * value)

    def window(number, _):
        way, slot = number // SLOTS, number % SLOTS
        turn, which = slot // 2, slot % 2
        corner = infos[way, turn, which, 0, 0]
        top = corner % TILE - way // 2 * TILE
        left = infos[way, turn, which, 0, 1] % TILE - way % 2 * TILE

        @pl.when((corner >= 0) & (top > -WIN) & (left > -WIN))
        def _():
            row0 = pl.multiple_of(jnp.clip(top // 8 * 8, 0, TILE - 520), 8)
            col0 = pl.multiple_of(jnp.clip(left // F * F, 0, TILE - 640), F)
            row = lax.broadcasted_iota(jnp.int32, (520, F), 0) + (row0 - top)
            in_row = (row >= 0) & (row < WIN)
            up = jnp.where(in_row & (row // 4 == lanes((520, F))), 1.0, 0.0)
            down = jnp.where(in_row, profile(row.astype(jnp.float32)), 0.0)
            col = lanes((F, 640)) + (col0 - left)
            in_col = (col >= 0) & (col < WIN)
            tap = lax.broadcasted_iota(jnp.int32, (F, 640), 0)
            across = jnp.where(in_col & (col // 4 == tap), 1.0, 0.0).astype(jnp.bfloat16)
            col = lanes((8, 640)) + (col0 - left)
            in_col = (col >= 0) & (col < WIN)
            side = jnp.where(in_col, profile(col.astype(jnp.float32)), 0.0)[0:1]
            tall = jnp.dot(
                up.astype(jnp.bfloat16), maps[way, slot], preferred_element_type=jnp.float32
            ).astype(jnp.bfloat16)
            for k in range(5):
                part = slice(k * F, (k + 1) * F)
                at = (pl.ds(row0, 520), pl.ds(pl.multiple_of(col0 + k * F, F), F))
                weight = down * side[:, part]
                value = jnp.dot(tall, across[:, part], preferred_element_type=jnp.float32)
                out_ref[at] += value * weight
                total[at] += weight
        return 0

    lax.fori_loop(0, 4 * SLOTS, window, 0)
    copies = []
    for k in range(TILE // F):
        part = slice(k * F, (k + 1) * F)
        out_ref[part, :] = out_ref[part, :] / jnp.maximum(total[part, :], 1.0)
        rows = pl.ds(k * F, F)
        copies.append(pltpu.make_async_copy(out_ref.at[rows], result.at[rows], sems.at[k]))
        copies[-1].start()
    for copy in copies:
        copy.wait()


def blend(infos, maps):
    return pl.pallas_call(
        blend_kernel,
        in_specs=[
            pl.BlockSpec(memory_space=pltpu.SMEM),
            pl.BlockSpec(memory_space=pltpu.VMEM),
        ],
        out_specs=pl.BlockSpec(memory_space=pltpu.HBM),
        scratch_shapes=[
            pltpu.VMEM((TILE, TILE), jnp.float32),
            pltpu.VMEM((TILE, TILE), jnp.float32),
            pltpu.SemaphoreType.DMA((TILE // F,)),
        ],
        out_shape=jax.ShapeDtypeStruct((TILE, TILE), jnp.float32),
        compiler_params=pltpu.CompilerParams(vmem_limit_bytes=40 << 20),
    )(infos, maps)


def share_kernel(maps, every, keep, send, recv):
    row, col = lax.axis_index("row"), lax.axis_index("col")
    rows, cols = lax.axis_size("row"), lax.axis_size("col")
    up, down, left, right = row > 0, row < rows - 1, col > 0, col < cols - 1
    own = pltpu.make_async_copy(maps, every.at[0], keep)
    own.start()
    goes = (right, down, down & right)
    comes = (left, up, up & left)
    barrier = pltpu.get_barrier_semaphore()
    for (by_row, by_col), out, back in zip(WAYS[1:], goes, comes):
        for sign, there in ((1, out), (-1, back)):
            @pl.when(there)
            def _():
                pl.semaphore_signal(
                    barrier, inc=1, device_id=(row + sign * by_row, col + sign * by_col),
                    device_id_type=MESH,
                )
    pl.semaphore_wait(barrier, sum(there.astype(jnp.int32) for there in goes + comes))
    copies = [
        pltpu.make_async_remote_copy(
            src_ref=maps, dst_ref=every.at[k], send_sem=send.at[k - 1], recv_sem=recv.at[k - 1],
            device_id=(row + WAYS[k][0], col + WAYS[k][1]), device_id_type=MESH,
        )
        for k in (1, 2, 3)
    ]
    for k in (2, 1, 0):
        pl.when(goes[k])(copies[k].start)
    own.wait()
    for k in range(3):
        pl.when(goes[k])(copies[k].wait_send)
        pl.when(comes[k])(copies[k].wait_recv)


def share(maps):
    return pl.pallas_call(
        share_kernel,
        out_shape=jax.ShapeDtypeStruct((4,) + maps.shape, maps.dtype),
        in_specs=[pl.BlockSpec(memory_space=pltpu.VMEM)],
        out_specs=pl.BlockSpec(memory_space=pltpu.VMEM),
        scratch_shapes=[
            pltpu.SemaphoreType.DMA,
            pltpu.SemaphoreType.DMA((3,)),
            pltpu.SemaphoreType.DMA((3,)),
        ],
        compiler_params=pltpu.CompilerParams(
            collective_id=1, has_side_effects=True, vmem_limit_bytes=40 << 20
        ),
    )(maps)


def local(scan, anchors, targets, *network):
    own = jnp.pad(anchors, ((0, 0), (0, 0), (0, 0), (0, F - 2)), constant_values=-1)
    framed, infos = frame(scan, own)
    maps, scores = networks(infos, targets, framed, *network)
    saliency = blend(infos, share(maps))
    return saliency, scores.reshape(targets.shape)


def solution(mesh):
    placed = (
        P("row", "col"),
        P(None, "row", "col", None),
        P(None, "row", "col"),
    ) + (P(),) * 8
    return jax.shard_map(
        local,
        mesh=mesh,
        in_specs=placed,
        out_specs=(P("row", "col"), P(None, "row", "col")),
        check_vma=False,
    )
```

```python
import jax
import jax.numpy as jnp
from jax import lax
from jax.experimental import pallas as pl
from jax.experimental.pallas import tpu as pltpu
from jax.sharding import PartitionSpec as P

TILE = 1024
WIN = 512
RIM = 512
C = 64
F = 128
SLOTS = 4
LOW = -3.0e38
MESH = pl.DeviceIdType.MESH
WAYS = ((0, 0), (0, 1), (1, 0), (1, 1))


def lanes(shape):
    return lax.broadcasted_iota(jnp.int32, shape, len(shape) - 1)


def frame_kernel(
    scan, own, framed, infos,
    raw, pixels, blank_rows, blank_cols, blanks, loads, keeps, up_send, up_recv, left_send, left_recv,
    corner_send, corner_recv, info_send, info_recv,
):
    row, col = lax.axis_index("row"), lax.axis_index("col")
    rows, cols = lax.axis_size("row"), lax.axis_size("col")
    up, down, left, right = row > 0, row < rows - 1, col > 0, col < cols - 1
    chunks = TILE // F
    fetch = [
        pltpu.make_async_copy(scan.at[pl.ds(k * F, F)], raw.at[pl.ds(k * F, F)], loads.at[k])
        for k in range(chunks)
    ]
    for copy in fetch:
        copy.start()
    infos[...] = jnp.full_like(infos, -1)
    infos[0] = own[...]

    blank_rows[...] = jnp.zeros_like(blank_rows)
    blank_cols[...] = jnp.zeros_like(blank_cols)

    def blank(source, k, by_rows, by_cols, there):
        return pltpu.make_async_copy(source, framed.at[by_rows, by_cols], blanks.at[k]), there

    edge, beyond = pl.ds(TILE, 16), pl.ds(TILE, F)
    no_down, no_right = row == rows - 1, col == cols - 1
    clears = (
        blank(blank_rows, 0, edge, pl.ds(0, TILE), no_down),
        blank(blank_rows.at[:, pl.ds(0, RIM)], 1, edge, pl.ds(TILE, RIM), no_down & right),
        blank(blank_cols, 2, pl.ds(0, TILE), beyond, no_right),
        blank(blank_cols.at[pl.ds(0, RIM)], 3, pl.ds(TILE, RIM), beyond, no_right),
    )
    for clear, there in clears:
        pl.when(there)(clear.start)

    barrier = pltpu.get_barrier_semaphore()
    partners = (
        (-1, 0, up), (1, 0, down), (0, -1, left), (0, 1, right),
        (1, 1, down & right), (-1, -1, up & left),
    )
    for by_row, by_col, there in partners:
        @pl.when(there)
        def _():
            pl.semaphore_signal(
                barrier, inc=1, device_id=(row + by_row, col + by_col), device_id_type=MESH
            )
    pl.semaphore_wait(barrier, sum(there.astype(jnp.int32) for _, _, there in partners))

    def remote(source, target, send, recv, by_row, by_col):
        return pltpu.make_async_remote_copy(
            src_ref=source, dst_ref=target, send_sem=send, recv_sem=recv,
            device_id=(row + by_row, col + by_col), device_id_type=MESH,
        )

    def part(k):
        return pl.ds(k * F, F)

    def under(k):
        return pl.ds(TILE + k * F, F)

    ups = [
        remote(pixels.at[part(k % 4), pl.ds(k // 4 * RIM, RIM)],
               framed.at[under(k % 4), pl.ds(k // 4 * RIM, RIM)],
               up_send.at[k], up_recv.at[k], -1, 0)
        for k in range(8)
    ]
    lefts = [
        remote(pixels.at[part(k), pl.ds(0, RIM)], framed.at[part(k), pl.ds(TILE, RIM)],
               left_send.at[k], left_recv.at[k], 0, -1)
        for k in range(chunks)
    ]
    corners = [
        remote(framed.at[under(k), pl.ds(0, RIM)], framed.at[under(k), pl.ds(TILE, RIM)],
               corner_send.at[k], corner_recv.at[k], 0, -1)
        for k in range(RIM // F)
    ]
    tells = [
        (remote(own, infos.at[1], info_send.at[0], info_recv.at[0], 0, 1), right, left),
        (remote(own, infos.at[2], info_send.at[1], info_recv.at[1], 1, 0), down, up),
        (remote(own, infos.at[3], info_send.at[2], info_recv.at[2], 1, 1), down & right, up & left),
    ]
    kept = [
        pltpu.make_async_copy(pixels.at[part(k)], framed.at[part(k), pl.ds(0, TILE)], keeps.at[k])
        for k in range(chunks)
    ]
    for k in range(chunks):
        fetch[k].wait()
        pixels[k * F : (k + 1) * F, :] = raw[k * F : (k + 1) * F, :].astype(jnp.bfloat16)
        if k < 4:
            pl.when(up)(ups[k].start)
        if k == 3:
            for late in ups[4:]:
                pl.when(up)(late.start)
        pl.when(left)(lefts[k].start)
        kept[k].start()
    for tell, goes, _ in tells:
        pl.when(goes)(tell.start)
    for k in range(len(ups)):
        pl.when(down)(ups[k].wait_recv)
        if k < len(corners):
            pl.when(down & left)(corners[k].start)
    for tell, goes, comes in tells:
        pl.when(goes)(tell.wait_send)
        pl.when(comes)(tell.wait_recv)
    for k in range(chunks):
        kept[k].wait()
        pl.when(left)(lefts[k].wait_send)
        pl.when(right)(lefts[k].wait_recv)
        pl.when(up)(ups[k].wait_send)
        if k < len(corners):
            pl.when(down & left)(corners[k].wait_send)
            pl.when(down & right)(corners[k].wait_recv)
    for clear, there in clears:
        pl.when(there)(clear.wait)


def frame(scan, own):
    chunks, rim = TILE // F, RIM // F
    sems = [4, chunks, chunks, 8, 8, chunks, chunks, rim, rim, 3, 3]
    return pl.pallas_call(
        frame_kernel,
        out_shape=[
            jax.ShapeDtypeStruct((TILE + RIM, TILE + RIM), jnp.bfloat16),
            jax.ShapeDtypeStruct((4,) + own.shape, jnp.int32),
        ],
        in_specs=[pl.BlockSpec(memory_space=pltpu.HBM), pl.BlockSpec(memory_space=pltpu.VMEM)],
        out_specs=[pl.BlockSpec(memory_space=pltpu.HBM), pl.BlockSpec(memory_space=pltpu.VMEM)],
        scratch_shapes=[
            pltpu.VMEM((TILE, TILE), jnp.float32),
            pltpu.VMEM((TILE, TILE), jnp.bfloat16),
            pltpu.VMEM((16, TILE), jnp.bfloat16),
            pltpu.VMEM((TILE, F), jnp.bfloat16),
        ] + [pltpu.SemaphoreType.DMA((n,)) for n in sems],
        compiler_params=pltpu.CompilerParams(
            collective_id=0, has_side_effects=True, vmem_limit_bytes=60 << 20
        ),
    )(scan, own)


def put_taps(ref, row, value):
    value = value.astype(jnp.bfloat16)
    lane = lanes((C, F))
    none = jnp.zeros((), jnp.bfloat16)
    ref[row, 0:C, :] = jnp.where(lane == 0, none, pltpu.roll(value, 1, 1))
    ref[row, C : 2 * C, :] = value
    ref[row, 2 * C : 3 * C, :] = jnp.where(lane == F - 1, none, pltpu.roll(value, F - 1, 1))


def convolved(taps_ref, weight_ref, finish):
    data = jnp.concatenate([taps_ref[k] for k in range(F)], 1)
    out = jnp.dot(weight_ref[...], data, preferred_element_type=jnp.float32)

    def part(tap, k):
        return out[tap * C : (tap + 1) * C, k * F : (k + 1) * F]

    for k in range(F):
        sums = part(1, k)
        if k > 0:
            sums = sums + part(0, k - 1)
        if k < F - 1:
            sums = sums + part(2, k + 1)
        finish(k, sums)


def arrange(stem_raw, first_raw, second_raw, biases_raw, stem_w, first_w, second_w, back_w, biases):
    taps = [stem_raw[k // 7, k % 7].astype(jnp.float32) for k in range(49)]
    turned = jnp.concatenate(taps, 0).T.astype(jnp.bfloat16)
    tap = lax.broadcasted_iota(jnp.int32, (49, 216), 0)
    tap_row, tap_col = tap // 7, tap % 7
    place_col, place_row = lanes((49, 216)) // 24, lanes((49, 216)) % 24
    for r in range(8):
        for q in range(2):
            hit = (place_row == 2 * r + tap_row) & (place_col == 2 * q + tap_col)
            hit = jnp.where(hit, 1.0, 0.0).astype(jnp.bfloat16)
            at = (r * 2 + q) * C
            stem_w[at : at + C, :] = jnp.dot(
                turned, hit, preferred_element_type=jnp.float32
            ).astype(jnp.bfloat16)
    for raw, laid in ((first_raw, first_w), (second_raw, second_w)):
        for dy in range(3):
            block = raw[dy * 3 : dy * 3 + 3].reshape(3 * C, C).astype(jnp.float32)
            laid[dy * C : (dy + 1) * C, :] = block.T.astype(jnp.bfloat16)
    for dy in range(3):
        blocks = [second_raw[(2 - dy) * 3 + (2 - dx)] for dx in range(3)]
        back_w[dy * C : (dy + 1) * C, :] = jnp.concatenate(blocks, 1)
    eye = lax.broadcasted_iota(jnp.int32, (C, C), 0) == lanes((C, C))
    for k in range(3):
        upright = jnp.sum(jnp.where(eye, biases_raw[k][...], 0.0), 1, keepdims=True)
        biases[k] = jnp.broadcast_to(upright, (C, F))


def net_kernel(
    infos, targets, source, stem_raw, first_raw, second_raw,
    stem_bias_raw, first_bias_raw, second_bias_raw, heads, head_bias,
    map_ref, logit_ref,
    stem_w, first_w, second_w, back_w, biases,
    pixels, spread_ref, picked, feats, hidden, grads, acc, order, arrival,
):
    count = jnp.int32(0)
    for slot in range(SLOTS):
        live = infos[0, slot // 2, slot % 2, 0, 0] >= 0

        @pl.when(live)
        def _():
            order[count] = slot

        count = count + live.astype(jnp.int32)

    def place(number):
        slot = order[number]
        turn, which = slot // 2, slot % 2
        top, left = (infos[0, turn, which, 0, k] % TILE for k in range(2))
        return slot, top, left, targets[turn, which, 0]

    def fetch(number):
        _, top, left, _ = place(number)
        row0 = pl.multiple_of(top // 16 * 16, 16)
        col0 = pl.multiple_of(left // F * F, F)
        here = number % 2
        return pltpu.make_async_copy(
            source.at[pl.ds(row0, 528), pl.ds(col0, 640)], pixels.at[here], arrival.at[here]
        )

    @pl.when(count > 0)
    def _():
        fetch(0).start()

    biases_raw = (stem_bias_raw, first_bias_raw, second_bias_raw)
    arrange(
        stem_raw, first_raw, second_raw, biases_raw, stem_w, first_w, second_w, back_w, biases
    )
    map_ref[...] = jnp.zeros_like(map_ref)
    for slot in range(SLOTS):
        logit_ref[slot] = jnp.float32(0.0)

    def window(number, _):
        slot, top, left, target = place(number)

        @pl.when(number + 1 < count)
        def _():
            fetch(number + 1).start()

        over = left % F
        lane = lanes((640, F))
        apart = lax.broadcasted_iota(jnp.int32, (640, F), 0) - over - lane * 4
        for u in range(9):
            hit = apart == u - 3
            if u < 3:
                hit = hit & (lane > 0)
            if u > 6:
                hit = hit & (lane < F - 1)
            spread_ref[:, u * F : (u + 1) * F] = jnp.where(hit, 1.0, 0.0).astype(jnp.bfloat16)
        below = top % 16
        row = lax.broadcasted_iota(jnp.int32, (520, 528), 0) - 3
        shift = jnp.where(
            (lanes((520, 528)) - below == row) & (row >= 0) & (row < WIN), 1.0, 0.0
        ).astype(jnp.bfloat16)
        fetch(number).wait()
        moved = jnp.dot(shift, pixels[number % 2], preferred_element_type=jnp.float32)
        picked[...] = jnp.dot(
            moved.astype(jnp.bfloat16), spread_ref[...], preferred_element_type=jnp.float32
        )
        stem_bias = biases[0]
        lane0 = lanes((C, F)) == 0
        none = jnp.zeros((), jnp.bfloat16)

        def stem():
            even = odd = jnp.full((C, F), LOW, jnp.float32)
            slabs = []
            for k in range(F // 4):
                slab = [
                    picked[k * 16 : k * 16 + 24, u * F : (u + 1) * F] for u in range(9)
                ]
                slabs.append(jnp.concatenate(slab, 0))
            data = jnp.concatenate(slabs, 1).astype(jnp.bfloat16)
            out = jnp.dot(stem_w[...], data, preferred_element_type=jnp.float32)
            for k in range(F // 4):
                for r in range(4):
                    part = lambda n: out[
                        (r * 4 + n) * C : (r * 4 + n + 1) * C, k * F : (k + 1) * F
                    ]
                    e_high = jnp.maximum(jnp.maximum(even, part(0)), part(2))
                    o_high = jnp.maximum(jnp.maximum(odd, part(1)), part(3))
                    even, odd = part(2), part(3)
                    high = jnp.maximum(e_high, o_high) + stem_bias
                    high = jnp.maximum(high, 0.0).astype(jnp.bfloat16)
                    side = jnp.maximum(o_high + stem_bias, 0.0).astype(jnp.bfloat16)
                    before = jnp.where(lane0, none, pltpu.roll(side, 1, 1))
                    put_taps(feats, k * 4 + r, jnp.maximum(high, before))

        stem()

        def after_first(row, sums):
            put_taps(hidden, row, jnp.maximum(sums + biases[1], 0.0))

        convolved(feats, first_w, after_first)

        eye = lax.broadcasted_iota(jnp.int32, (C, C), 0) == lanes((C, C))
        wanted = lax.broadcasted_iota(jnp.int32, (9, C), 0) == target
        head = jnp.where(wanted, heads[...].astype(jnp.float32), 0.0)
        head = jnp.sum(head, 0, keepdims=True)
        column = jnp.sum(jnp.where(eye, head, 0.0), 1, keepdims=True)
        grad = jnp.broadcast_to(
            (column / float(F * F)).astype(jnp.bfloat16).astype(jnp.float32), (C, F)
        )
        acc[...] = jnp.zeros_like(acc)
        held = []

        def after_second(row, sums):
            value = sums + feats[row, C : 2 * C, :].astype(jnp.float32) + biases[2]
            value = jnp.maximum(value, 0.0)
            out = jnp.where(value > 0, grad, 0.0)
            put_taps(grads, row, out)
            held.append((value, out))
            if len(held) == 4:
                acc[0] += sum(kept for kept, _ in held)
                acc[1] += sum(kept for _, kept in held)
                held.clear()

        convolved(hidden, second_w, after_second)

        def after_back(row, sums):
            open_ = hidden[row, C : 2 * C, :].astype(jnp.float32) > 0
            value = jnp.where(open_, sums, 0.0).astype(jnp.bfloat16).astype(jnp.float32)
            if row == 0:
                acc[3] = value
            if row == F - 1:
                acc[4] = value
            held.append(value)
            if len(held) == 4:
                acc[2] += sum(held)
                held.clear()

        convolved(grads, back_w, after_back)

        mean = jnp.sum(acc[0], 1, keepdims=True) / float(F * F)
        logit = jnp.sum(mean * column)
        bias = jnp.sum(jnp.where(lanes((1, 9)) == target, head_bias[...], 0.0))
        logit_ref[slot] = logit + bias

        whole = acc[2]
        parts = [whole - acc[4], whole, whole - acc[3]]
        lane = lanes((C, F))
        channel = jnp.sum(acc[1], 1, keepdims=True)
        for dy in range(3):
            for dx in range(3):
                drop = {0: F - 1, 1: F, 2: 0}[dx]
                total = jnp.sum(jnp.where(lane == drop, 0.0, parts[dy]), 1, keepdims=True)
                flat = jnp.sum(jnp.where(eye, total, 0.0), 0, keepdims=True)
                weight = first_raw[(2 - dy) * 3 + (2 - dx)].astype(jnp.float32)
                channel = channel + jnp.sum(weight * flat, 1, keepdims=True)
        channel = jnp.broadcast_to(channel, (C, F))

        def rows(step, _):
            base = pl.multiple_of(step * 16, 16)
            found = [
                jnp.sum(
                    feats[base + k, C : 2 * C, :].astype(jnp.float32) * channel, 0, keepdims=True
                )
                for k in range(16)
            ]
            found = jnp.maximum(jnp.concatenate(found, 0), 0.0)
            map_ref[slot, pl.ds(base, 16), :] = found.astype(jnp.bfloat16)
            return 0

        lax.fori_loop(0, F // 16, rows, 0)
        return 0

    lax.fori_loop(0, count, window, 0)


def networks(infos, targets, framed, stem_weight, stem_bias, conv1_weight, conv1_bias, conv2_weight,
             conv2_bias, head_weight, head_bias):
    biases = [bias.reshape(1, C) for bias in (stem_bias, conv1_bias, conv2_bias)]
    whole = pl.BlockSpec(memory_space=pltpu.VMEM)
    maps, logits = pl.pallas_call(
        net_kernel,
        in_specs=[pl.BlockSpec(memory_space=pltpu.SMEM)] * 2
        + [pl.BlockSpec(memory_space=pltpu.HBM)] + [whole] * 8,
        out_specs=[whole, pl.BlockSpec(memory_space=pltpu.SMEM)],
        scratch_shapes=[
            pltpu.VMEM((16 * C, 216), jnp.bfloat16),
            pltpu.VMEM((3 * C, 3 * C), jnp.bfloat16),
            pltpu.VMEM((3 * C, 3 * C), jnp.bfloat16),
            pltpu.VMEM((3 * C, 3 * C), jnp.bfloat16),
            pltpu.VMEM((3, C, F), jnp.float32),
            pltpu.VMEM((2, 528, 640), jnp.bfloat16),
            pltpu.VMEM((640, 9 * F), jnp.bfloat16),
            pltpu.VMEM((520, 9 * F), jnp.float32),
            pltpu.VMEM((F, 3 * C, F), jnp.bfloat16),
            pltpu.VMEM((F, 3 * C, F), jnp.bfloat16),
            pltpu.VMEM((F, 3 * C, F), jnp.bfloat16),
            pltpu.VMEM((5, C, F), jnp.float32),
            pltpu.SMEM((SLOTS,), jnp.int32),
            pltpu.SemaphoreType.DMA((2,)),
        ],
        out_shape=[
            jax.ShapeDtypeStruct((SLOTS, F, F), jnp.bfloat16),
            jax.ShapeDtypeStruct((SLOTS,), jnp.float32),
        ],
        compiler_params=pltpu.CompilerParams(vmem_limit_bytes=58 << 20),
    )(
        infos, targets, framed, stem_weight, conv1_weight.reshape(9, C, C),
        conv2_weight.reshape(9, C, C), *biases, head_weight.T, head_bias.reshape(1, 9),
    )
    return maps, logits


def blend_kernel(infos, maps, result, out_ref, total, sems):
    out_ref[...] = jnp.zeros_like(out_ref)
    total[...] = jnp.zeros_like(total)

    def profile(offset):
        value = (offset - (WIN - 1) / 2.0) * (1.0 / (WIN / 4.0))
        return jnp.exp(-0.5 * value * value)

    def window(number, _):
        way, slot = number // SLOTS, number % SLOTS
        turn, which = slot // 2, slot % 2
        corner = infos[way, turn, which, 0, 0]
        top = corner % TILE - way // 2 * TILE
        left = infos[way, turn, which, 0, 1] % TILE - way % 2 * TILE

        @pl.when((corner >= 0) & (top > -WIN) & (left > -WIN))
        def _():
            row0 = pl.multiple_of(jnp.clip(top // 8 * 8, 0, TILE - 520), 8)
            col0 = pl.multiple_of(jnp.clip(left // F * F, 0, TILE - 640), F)
            row = lax.broadcasted_iota(jnp.int32, (520, F), 0) + (row0 - top)
            in_row = (row >= 0) & (row < WIN)
            up = jnp.where(in_row & (row // 4 == lanes((520, F))), 1.0, 0.0)
            down = jnp.where(in_row, profile(row.astype(jnp.float32)), 0.0)
            col = lanes((F, 640)) + (col0 - left)
            in_col = (col >= 0) & (col < WIN)
            tap = lax.broadcasted_iota(jnp.int32, (F, 640), 0)
            across = jnp.where(in_col & (col // 4 == tap), 1.0, 0.0).astype(jnp.bfloat16)
            col = lanes((8, 640)) + (col0 - left)
            in_col = (col >= 0) & (col < WIN)
            side = jnp.where(in_col, profile(col.astype(jnp.float32)), 0.0)[0:1]
            tall = jnp.dot(
                up.astype(jnp.bfloat16), maps[way, slot], preferred_element_type=jnp.float32
            ).astype(jnp.bfloat16)
            for k in range(5):
                part = slice(k * F, (k + 1) * F)
                at = (pl.ds(row0, 520), pl.ds(pl.multiple_of(col0 + k * F, F), F))
                weight = down * side[:, part]
                value = jnp.dot(tall, across[:, part], preferred_element_type=jnp.float32)
                out_ref[at] += value * weight
                total[at] += weight
        return 0

    lax.fori_loop(0, 4 * SLOTS, window, 0)
    copies = []
    for k in range(TILE // F):
        part = slice(k * F, (k + 1) * F)
        out_ref[part, :] = out_ref[part, :] / jnp.maximum(total[part, :], 1.0)
        rows = pl.ds(k * F, F)
        copies.append(pltpu.make_async_copy(out_ref.at[rows], result.at[rows], sems.at[k]))
        copies[-1].start()
    for copy in copies:
        copy.wait()


def blend(infos, maps):
    return pl.pallas_call(
        blend_kernel,
        in_specs=[
            pl.BlockSpec(memory_space=pltpu.SMEM),
            pl.BlockSpec(memory_space=pltpu.VMEM),
        ],
        out_specs=pl.BlockSpec(memory_space=pltpu.HBM),
        scratch_shapes=[
            pltpu.VMEM((TILE, TILE), jnp.float32),
            pltpu.VMEM((TILE, TILE), jnp.float32),
            pltpu.SemaphoreType.DMA((TILE // F,)),
        ],
        out_shape=jax.ShapeDtypeStruct((TILE, TILE), jnp.float32),
        compiler_params=pltpu.CompilerParams(vmem_limit_bytes=40 << 20),
    )(infos, maps)


def share_kernel(maps, every, keep, send, recv):
    row, col = lax.axis_index("row"), lax.axis_index("col")
    rows, cols = lax.axis_size("row"), lax.axis_size("col")
    up, down, left, right = row > 0, row < rows - 1, col > 0, col < cols - 1
    own = pltpu.make_async_copy(maps, every.at[0], keep)
    own.start()
    goes = (right, down, down & right)
    comes = (left, up, up & left)
    barrier = pltpu.get_barrier_semaphore()
    for (by_row, by_col), out, back in zip(WAYS[1:], goes, comes):
        for sign, there in ((1, out), (-1, back)):
            @pl.when(there)
            def _():
                pl.semaphore_signal(
                    barrier, inc=1, device_id=(row + sign * by_row, col + sign * by_col),
                    device_id_type=MESH,
                )
    pl.semaphore_wait(barrier, sum(there.astype(jnp.int32) for there in goes + comes))
    copies = [
        pltpu.make_async_remote_copy(
            src_ref=maps, dst_ref=every.at[k], send_sem=send.at[k - 1], recv_sem=recv.at[k - 1],
            device_id=(row + WAYS[k][0], col + WAYS[k][1]), device_id_type=MESH,
        )
        for k in (1, 2, 3)
    ]
    for k in (2, 1, 0):
        pl.when(goes[k])(copies[k].start)
    own.wait()
    for k in range(3):
        pl.when(goes[k])(copies[k].wait_send)
        pl.when(comes[k])(copies[k].wait_recv)


def share(maps):
    return pl.pallas_call(
        share_kernel,
        out_shape=jax.ShapeDtypeStruct((4,) + maps.shape, maps.dtype),
        in_specs=[pl.BlockSpec(memory_space=pltpu.VMEM)],
        out_specs=pl.BlockSpec(memory_space=pltpu.VMEM),
        scratch_shapes=[
            pltpu.SemaphoreType.DMA,
            pltpu.SemaphoreType.DMA((3,)),
            pltpu.SemaphoreType.DMA((3,)),
        ],
        compiler_params=pltpu.CompilerParams(
            collective_id=1, has_side_effects=True, vmem_limit_bytes=40 << 20
        ),
    )(maps)


def local(scan, anchors, targets, *network):
    own = jnp.pad(anchors, ((0, 0), (0, 0), (0, 0), (0, F - 2)), constant_values=-1)
    framed, infos = frame(scan, own)
    maps, scores = networks(infos, targets, framed, *network)
    saliency = blend(infos, share(maps))
    return saliency, scores.reshape(targets.shape)


def solution(mesh):
    placed = (
        P("row", "col"),
        P(None, "row", "col", None),
        P(None, "row", "col"),
    ) + (P(),) * 8
    return jax.shard_map(
        local,
        mesh=mesh,
        in_specs=placed,
        out_specs=(P("row", "col"), P(None, "row", "col")),
        check_vma=False,
    )
```
